32 devices in a mesh: groups: 2 (over x), seq: 8 (over z, y), head: 2 (over core).
Axes of the slice: x: 2, y: 2, z: 4, core: 2. Of those that a mesh axis runs over, the one named last changes fastest.
Arguments:
- queries: bfloat16 [8192, 2048], P(('groups', 'seq'), 'head'), parts along dimension 0, may hold values from -6 to 6
- keys: bfloat16 [8192, 1024], P(('groups', 'seq'), 'head'), parts along dimension 0, may hold values from -6 to 6
- values: bfloat16 [8192, 1024], P(('groups', 'seq'), 'head'), parts along dimension 0, may hold values from -6 to 6
- segments: int32 [8192], P('groups'), parts along dimension 0, may hold values from 0 to 7, never falling along the last dimension, each value on 1 to 1024 neighbouring positions
- out_weight: bfloat16 [2048, 5376], P('head'), may hold values from -0.125 to 0.125
Outputs:
- mixed: bfloat16 [8192, 5376], P(('groups', 'seq')), parts along dimension 0
The draws below stay inside these ranges and needn't reach their ends.
There are 2 independent parts, one for each index of `groups`. The reference program is written for one: setup_inputs(seed, part) draws one part's arguments, and reference() takes and returns one part's arrays. A program takes and returns all parts, laid end to end along the dimension named above; an argument that names none is the same for every part. Nothing has to cross between parts.
Inputs may be any that keep to these rules, and one draw needn't show every extreme that they name: `segments`: document ids never fall along the slab; each document has 1 to 1024 tokens, one exactly 1024.
All inputs are finite; a program needn't handle non-finite values.
Results may differ from the reference program's by a relative error of at most 0.011.
Values may be sent and summed in bfloat16 or wider, within the bound.
No kernel may reach another device: no remote copies, remote signals or barrier semaphores. Data moves between devices by JAX's collectives and lax.ppermute only.
A program may use at most 128 MiB of HBM per device.

```python
import math
import jax
import jax.numpy as jnp
import numpy as np
from jax import lax

D = 5376
QUERY_HEADS = 16
KEY_VALUE_HEADS = 8
HEAD_SIZE = 128
SCALAR = 168
ATTENTION_SPAN = 1024
SLAB_TOKENS = 4096


def draw_keys(key, part):
    final_output = jnp.clip(jax.random.normal(jax.random.fold_in(key, 11), (SLAB_TOKENS, KEY_VALUE_HEADS * HEAD_SIZE), jnp.float32), -6.0, 6.0)
    return final_output.astype(jnp.bfloat16)


def draw_queries(key, part):
    final_output = jnp.clip(jax.random.normal(jax.random.fold_in(key, 21), (SLAB_TOKENS, QUERY_HEADS * HEAD_SIZE), jnp.float32), -6.0, 6.0)
    return final_output.astype(jnp.bfloat16)


def shard_levels(rng, extent, pieces, least, largest):
    def one(position, parts):
        steps = jax.random.uniform(jax.random.fold_in(jax.random.fold_in(rng, 6), position), (parts,), jnp.float32, least / len(pieces), largest / len(pieces))
        return jnp.repeat(jnp.exp(steps), extent[position] // parts).reshape((-1,) + (1,) * (len(extent) - position - 1))

    loudness = one(*pieces[0])
    for cut in pieces[1:]:
        loudness = loudness * one(*cut)
    return loudness


def profile(amount, total, limit, skew):
    loads = [(1 << 20) // math.isqrt(rank ** skew) + 1 for rank in range(2, amount + 1)]
    rest, holding = total - limit - (amount - 1), [1] * (amount - 1)
    while rest > 0:
        candidates = [i for i in range(amount - 1) if holding[i] < limit]
        mass, remaining = sum([loads[i] for i in candidates]), rest
        for i in candidates:
            extra = min(limit - holding[i], max(1, remaining * loads[i] // mass), rest)
            holding[i] = holding[i] + extra
            rest = rest - extra
    return np.array([limit] + holding)


def uneven_parts(key, amount, total, reach, skew):
    if amount == 2:
        one = jax.random.randint(key, (), max(1, total - reach), min(reach, total - 1) + 1)
        return jnp.stack([one, total - one])
    sizes = jnp.asarray(profile(amount, total, reach, skew), jnp.int32)
    pairs = (amount - 1) // 2
    giver, receiver = sizes[1:1 + 2 * pairs:2], sizes[2:2 + 2 * pairs:2]
    margin = jnp.minimum(giver - 1, reach - receiver)
    passed = jax.random.randint(jax.random.fold_in(key, 1), (pairs,), 0, 1 << 20) % (margin + 1)
    sizes = sizes.at[1:1 + 2 * pairs:2].set(giver - passed).at[2:2 + 2 * pairs:2].set(receiver + passed)
    return sizes[jax.random.permutation(jax.random.fold_in(key, 2), amount)]


def noise(own_key, shape, width, reach, cuts=(), held_as=jnp.bfloat16):
    loudness = shard_levels(own_key, shape, cuts, -0.22, 0.18) if cuts else 1.0
    array = jax.random.normal(own_key, shape, jnp.float32) * width * loudness
    return jnp.minimum(jnp.maximum(array, -reach), reach).astype(held_as)


def setup_inputs(seed: int = 0, part: int = 0) -> dict:
    seeds = jax.random.split(jax.random.key(seed), 6)
    part_splits = jax.random.split(jax.random.fold_in(seeds[5], part), 6)
    queries = draw_queries(jax.random.fold_in(jax.random.fold_in(seeds[5], part), 71), part)
    keys = draw_keys(jax.random.fold_in(jax.random.fold_in(seeds[5], part), 71), part)
    values = noise(part_splits[2], (SLAB_TOKENS, KEY_VALUE_HEADS * HEAD_SIZE), 1.0, 6.0, ((0, 8), (1, 2)))
    segments = jnp.searchsorted(jnp.cumsum(uneven_parts(part_splits[3], 8, SLAB_TOKENS, SLAB_TOKENS // 4, 2)), jnp.arange(SLAB_TOKENS), side="right").astype(jnp.int32)
    out_weight = noise(seeds[4], (QUERY_HEADS * HEAD_SIZE, D), (QUERY_HEADS * HEAD_SIZE) ** -0.5, 0.125, ((0, 2),))
    return {"queries": queries, "keys": keys, "values": values, "segments": segments, "out_weight": out_weight}


def reference(queries, keys, values, segments, out_weight):
    query_group = QUERY_HEADS // KEY_VALUE_HEADS
    token_block = math.gcd(SLAB_TOKENS, 512)
    window_span = ATTENTION_SPAN + token_block
    padded_keys = jnp.concatenate([jnp.zeros((ATTENTION_SPAN, KEY_VALUE_HEADS * HEAD_SIZE), keys.dtype), keys])
    padded_values = jnp.concatenate([jnp.zeros((ATTENTION_SPAN, KEY_VALUE_HEADS * HEAD_SIZE), values.dtype), values])
    pad_segments = jnp.concatenate([jnp.full((ATTENTION_SPAN,), -1, jnp.int32), segments.astype(jnp.int32)])

    def one_block(block_id):
        first_index = (block_id * token_block).astype(jnp.int32)
        query_matrix_rows = lax.dynamic_slice_in_dim(queries, first_index, token_block, 0).astype(jnp.float32).reshape(token_block, KEY_VALUE_HEADS, query_group, HEAD_SIZE)
        key_matrix_rows = lax.dynamic_slice_in_dim(padded_keys, first_index, window_span, 0).astype(jnp.float32).reshape(window_span, KEY_VALUE_HEADS, HEAD_SIZE)
        value_matrix_rows = lax.dynamic_slice_in_dim(padded_values, first_index, window_span, 0).astype(jnp.float32).reshape(window_span, KEY_VALUE_HEADS, HEAD_SIZE)
        seg_query = lax.dynamic_slice_in_dim(segments.astype(jnp.int32), first_index, token_block, 0)
        seg_key = lax.dynamic_slice_in_dim(pad_segments, first_index, window_span, 0)
        query_pos = first_index + jnp.arange(token_block, dtype=jnp.int32)
        key_pos = first_index - ATTENTION_SPAN + jnp.arange(window_span, dtype=jnp.int32)
        allowed = (key_pos[None, :] <= query_pos[:, None]) & (query_pos[:, None] - key_pos[None, :] < ATTENTION_SPAN) & (seg_key[None, :] == seg_query[:, None])
        scores = jnp.einsum('qkgd,pkd->kgqp', query_matrix_rows, key_matrix_rows) * (SCALAR ** -0.5)
        masked = jnp.where(allowed, scores, -1e30)
        row_max = jnp.max(masked, axis=-1, keepdims=True)
        expo = jnp.where(allowed, jnp.exp(masked - row_max), 0.0)
        weights = (expo / jnp.sum(expo, axis=-1, keepdims=True)).astype(jnp.bfloat16)
        heads_out = jnp.einsum('kgqp,pkd->qkgd', weights.astype(jnp.float32), value_matrix_rows)
        return heads_out.astype(jnp.bfloat16).reshape(token_block, QUERY_HEADS * HEAD_SIZE)

    attended = lax.map(one_block, jnp.arange(SLAB_TOKENS // token_block, dtype=jnp.int32)).reshape(SLAB_TOKENS, QUERY_HEADS * HEAD_SIZE)
    return jnp.dot(attended, out_weight, preferred_element_type=jnp.float32).astype(jnp.bfloat16)
```

```python
import jax
import jax.numpy as jnp
from jax import lax
from jax.experimental import pallas as pl
from jax.experimental.pallas import tpu as pltpu
from jax.sharding import PartitionSpec as P

HEAD_SIZE = 128
SCALAR = 168
ATTENTION_SPAN = 1024
TILE = 128
MARK = 128.0
LOG2E = 1.4426950408889634
MIB = 1 << 20


def joined(*parts):
    parts = [part for part in parts if part.shape[1]]
    return parts[0] if len(parts) == 1 else jnp.concatenate(parts, axis=1)


def attend_kernel(q_ref, own_ref, near_ref, far_ref, mark_ref, out_ref):
    rows = own_ref.shape[0]
    group = q_ref.shape[1] // HEAD_SIZE
    factor = LOG2E * SCALAR ** (-0.5)
    ones = jnp.ones((rows, HEAD_SIZE), jnp.bfloat16)

    def keys_of(ref, block):
        marks = mark_ref[block * rows : (block + 1) * rows, :]
        return jnp.concatenate([ref[:, :HEAD_SIZE], marks], axis=1)

    def values_of(ref):
        return jnp.concatenate([ref[:, HEAD_SIZE:], ones], axis=1)

    keys = [keys_of(far_ref, 0), keys_of(near_ref, 1), keys_of(own_ref, 2)]
    values = [values_of(far_ref), values_of(near_ref), values_of(own_ref)]
    row = lax.broadcasted_iota(jnp.int32, (TILE, TILE), 0)
    col = lax.broadcasted_iota(jnp.int32, (TILE, TILE), 1)
    inside = jnp.concatenate([col > row] * group, axis=0)
    causal = jnp.concatenate([col <= row] * group, axis=0)
    for t in range(rows // TILE):
        span = slice(t * TILE, (t + 1) * TILE)
        marks = mark_ref[2 * rows + t * TILE : 2 * rows + (t + 1) * TILE, :]
        query = jnp.concatenate(
            [
                jnp.concatenate([q_ref[span, g * HEAD_SIZE : (g + 1) * HEAD_SIZE], marks], axis=1)
                for g in range(group)
            ],
            axis=0,
        )
        parts = [
            (keys[0][t * TILE :], values[0][t * TILE :]),
            (keys[1], values[1]),
            (keys[2][: (t + 1) * TILE], values[2][: (t + 1) * TILE]),
        ]
        scores = [
            lax.dot_general(
                query, key, (((1,), (1,)), ((), ())), preferred_element_type=jnp.float32
            )
            for key, _ in parts
        ]
        first = jnp.where(inside, scores[0][:, :TILE], -1e30)
        scores[0] = joined(first, *([scores[0][:, TILE:]] if scores[0].shape[1] > TILE else []))
        last = jnp.where(causal, scores[2][:, t * TILE :], -1e30)
        scores[2] = joined(*([scores[2][:, : t * TILE]] if t else []), last)
        top = jnp.maximum(
            jnp.maximum(
                jnp.max(scores[0], axis=1, keepdims=True),
                jnp.max(scores[1], axis=1, keepdims=True),
            ),
            jnp.max(scores[2], axis=1, keepdims=True),
        )
        total = None
        for score, (_, value) in zip(scores, parts):
            weight = jnp.exp2((score - top) * factor).astype(jnp.bfloat16)
            term = jnp.dot(weight, value, preferred_element_type=jnp.float32)
            total = term if total is None else total + term
        result = (total[:, :HEAD_SIZE] / total[:, HEAD_SIZE:]).astype(jnp.bfloat16)
        for g in range(group):
            out_ref[span, g * HEAD_SIZE : (g + 1) * HEAD_SIZE] = result[
                g * TILE : (g + 1) * TILE
            ]


def attend(queries, own, near, far, marks, head):
    rows = own.shape[0]
    heads_kv = queries.shape[1] // 256
    width = queries.shape[1] // heads_kv
    whole = lambda a: pl.BlockSpec(a.shape, lambda i: (0,) * a.ndim)
    return pl.pallas_call(
        attend_kernel,
        grid=(1,),
        in_specs=[
            pl.BlockSpec((rows, width), lambda i: (0, head)),
            whole(own),
            whole(near),
            whole(far),
            whole(marks),
        ],
        out_specs=pl.BlockSpec((rows, width), lambda i: (0, 0)),
        out_shape=jax.ShapeDtypeStruct((rows, width), jnp.bfloat16),
        compiler_params=pltpu.CompilerParams(vmem_limit_bytes=12 * MIB),
        cost_estimate=pl.CostEstimate(
            flops=4 * 1024 * 1152 * 256, bytes_accessed=2 * MIB, transcendentals=1024 * 1152
        ),
    )(queries, own, near, far, marks)


def project_kernel(core_ref, *refs, pieces, has_base):
    own, other = refs[:pieces], refs[pieces : 2 * pieces]
    own_w, other_w = refs[2 * pieces], refs[2 * pieces + 1]
    base_ref = refs[2 * pieces + 2] if has_base else None
    out_ref = refs[-1]

    def run(sides):
        total = base_ref[...] if has_base else None
        for arrays, weight in sides:
            for i, array in enumerate(arrays):
                depth = array.shape[1]
                term = jnp.dot(
                    array[...],
                    weight[i * depth : (i + 1) * depth, :],
                    preferred_element_type=jnp.float32,
                )
                total = term if total is None else total + term
        out_ref[...] = total.astype(out_ref.dtype)

    @pl.when(core_ref[0] == 0)
    def _():
        run([(own, own_w), (other, other_w)])

    @pl.when(core_ref[0] != 0)
    def _():
        run([(other, other_w), (own, own_w)])


def project(core, own, other, own_w, other_w, row_block, base, dtype):
    rows, depth = own[0].shape
    pieces = len(own)
    columns = own_w.shape[1]
    tile = 768 if columns % 768 == 0 else 128
    small = pl.BlockSpec((rows, depth), lambda n, c: (0, 0))
    weight = pl.BlockSpec((pieces * depth, tile), lambda n, c: (row_block, n))
    block = pl.BlockSpec((rows, tile), lambda n, c: (0, n))
    has_base = base is not None
    return pl.pallas_call(
        lambda *refs: project_kernel(*refs, pieces=pieces, has_base=has_base),
        grid_spec=pltpu.PrefetchScalarGridSpec(
            num_scalar_prefetch=1,
            grid=(columns // tile,),
            in_specs=[small] * (2 * pieces) + [weight, weight] + [block] * has_base,
            out_specs=block,
        ),
        out_shape=jax.ShapeDtypeStruct((rows, columns), dtype),
        compiler_params=pltpu.CompilerParams(vmem_limit_bytes=24 * MIB),
        cost_estimate=pl.CostEstimate(
            flops=4 * rows * pieces * depth * columns,
            bytes_accessed=16 * MIB,
            transcendentals=0,
        ),
    )(core, *own, *other, own_w, other_w, *([base] if has_base else []))


def shards(queries, keys, values, segments, out_weight):
    rows = queries.shape[0]
    heads_kv = keys.shape[1] // HEAD_SIZE
    peers = lax.axis_size("seq")
    seq_index = lax.axis_index("seq")
    core = lax.axis_index("head").astype(jnp.int32).reshape(1)
    swap = [(0, 1), (1, 0)]

    def packed(h):
        part = slice(h * HEAD_SIZE, (h + 1) * HEAD_SIZE)
        return jnp.concatenate([keys[:, part], values[:, part]], axis=1)

    own = [packed(h) for h in range(heads_kv)]
    two_on = [(i, i + 2) for i in range(peers - 2)]
    one_on = [(i, i + 1) for i in range(peers - 1)]
    pair = [(i, i ^ 1) for i in range(peers)]
    odd = seq_index % 2 == 1
    far = [lax.ppermute(x, "seq", two_on) for x in own]
    near = [
        lax.ppermute(jnp.where(odd, f, x), "seq", pair) for f, x in zip(far[:-1], own[:-1])
    ]
    near.append(lax.ppermute(own[-1], "seq", one_on))
    other_w = lax.ppermute(out_weight, "head", swap)

    halo = 2 * rows
    padded = jnp.concatenate([jnp.full((halo,), -1, jnp.int32), segments])
    seen = lax.dynamic_slice_in_dim(padded, seq_index * rows, halo + rows, 0)
    ids = lax.broadcasted_iota(jnp.int32, (halo + rows, HEAD_SIZE), 1)
    marks = jnp.where(seen[:, None] == ids, MARK, 0.0).astype(jnp.bfloat16)

    mine = [
        attend(queries, own[h], near[h], far[h], marks, h) for h in range(heads_kv)
    ]
    theirs = [lax.ppermute(x, "head", swap) for x in mine]
    half = heads_kv // 2
    base = project(
        core, mine[:half], theirs[:half], out_weight, other_w, 0, None, jnp.float32
    )
    return project(
        core, mine[half:], theirs[half:], out_weight, other_w, 1, base, jnp.bfloat16
    )


def solution(mesh):
    placed = (
        P(("groups", "seq"), "head"),
        P(("groups", "seq"), "head"),
        P(("groups", "seq"), "head"),
        P("groups"),
        P("head", None),
    )
    return jax.shard_map(
        shards, mesh=mesh, in_specs=placed, out_specs=P(("groups", "seq"), None), check_vma=False
    )
```

```python
import jax
import jax.numpy as jnp
from jax import lax
from jax.experimental import pallas as pl
from jax.experimental.pallas import tpu as pltpu
from jax.sharding import PartitionSpec as P

HEAD_SIZE = 128
SCALAR = 168
ATTENTION_SPAN = 1024
TILE = 128
MARK = 128.0
LOG2E = 1.4426950408889634
MIB = 1 << 20


def joined(*parts):
    parts = [part for part in parts if part.shape[1]]
    return parts[0] if len(parts) == 1 else jnp.concatenate(parts, axis=1)


def attend_kernel(q_ref, own_ref, near_ref, far_ref, mark_ref, out_ref):
    rows = own_ref.shape[0]
    group = q_ref.shape[1] // HEAD_SIZE
    factor = LOG2E * SCALAR ** (-0.5)
    ones = jnp.ones((rows, HEAD_SIZE), jnp.bfloat16)

    def keys_of(ref, block):
        marks = mark_ref[block * rows : (block + 1) * rows, :]
        return jnp.concatenate([ref[:, :HEAD_SIZE], marks], axis=1)

    def values_of(ref):
        return jnp.concatenate([ref[:, HEAD_SIZE:], ones], axis=1)

    keys = [keys_of(far_ref, 0), keys_of(near_ref, 1), keys_of(own_ref, 2)]
    values = [values_of(far_ref), values_of(near_ref), values_of(own_ref)]
    row = lax.broadcasted_iota(jnp.int32, (TILE, TILE), 0)
    col = lax.broadcasted_iota(jnp.int32, (TILE, TILE), 1)
    inside = jnp.concatenate([col > row] * group, axis=0)
    causal = jnp.concatenate([col <= row] * group, axis=0)
    for t in range(rows // TILE):
        span = slice(t * TILE, (t + 1) * TILE)
        marks = mark_ref[2 * rows + t * TILE : 2 * rows + (t + 1) * TILE, :]
        query = jnp.concatenate(
            [
                jnp.concatenate([q_ref[span, g * HEAD_SIZE : (g + 1) * HEAD_SIZE], marks], axis=1)
                for g in range(group)
            ],
            axis=0,
        )
        parts = [
            (keys[0][t * TILE :], values[0][t * TILE :]),
            (keys[1], values[1]),
            (keys[2][: (t + 1) * TILE], values[2][: (t + 1) * TILE]),
        ]
        scores = [
            lax.dot_general(
                query, key, (((1,), (1,)), ((), ())), preferred_element_type=jnp.float32
            )
            for key, _ in parts
        ]
        first = jnp.where(inside, scores[0][:, :TILE], -1e30)
        scores[0] = joined(first, *([scores[0][:, TILE:]] if scores[0].shape[1] > TILE else []))
        last = jnp.where(causal, scores[2][:, t * TILE :], -1e30)
        scores[2] = joined(*([scores[2][:, : t * TILE]] if t else []), last)
        top = jnp.maximum(
            jnp.maximum(
                jnp.max(scores[0], axis=1, keepdims=True),
                jnp.max(scores[1], axis=1, keepdims=True),
            ),
            jnp.max(scores[2], axis=1, keepdims=True),
        )
        total = None
        for score, (_, value) in zip(scores, parts):
            weight = jnp.exp2((score - top) * factor).astype(jnp.bfloat16)
            term = jnp.dot(weight, value, preferred_element_type=jnp.float32)
            total = term if total is None else total + term
        result = (total[:, :HEAD_SIZE] / total[:, HEAD_SIZE:]).astype(jnp.bfloat16)
        for g in range(group):
            out_ref[span, g * HEAD_SIZE : (g + 1) * HEAD_SIZE] = result[
                g * TILE : (g + 1) * TILE
            ]


def in_vmem(x):
    return pltpu.with_memory_space_constraint(x, pltpu.VMEM)


def in_hbm(x):
    return pltpu.with_memory_space_constraint(x, pltpu.HBM)


def pack_kernel(keys_ref, values_ref, *refs):
    outs, sem = refs[:-1], refs[-1]
    copies = []
    for h, out in enumerate(outs):
        for side, ref in enumerate((keys_ref, values_ref)):
            copies.append(
                pltpu.make_async_copy(
                    ref.at[:, h * HEAD_SIZE : (h + 1) * HEAD_SIZE],
                    out.at[:, side * HEAD_SIZE : (side + 1) * HEAD_SIZE],
                    sem.at[h, side],
                )
            )
    for copy in copies:
        copy.start()
    for copy in copies:
        copy.wait()


def pack(keys, values):
    rows, heads = keys.shape[0], keys.shape[1] // HEAD_SIZE
    return pl.pallas_call(
        pack_kernel,
        in_specs=[pl.BlockSpec(memory_space=pltpu.HBM)] * 2,
        out_specs=[pl.BlockSpec(memory_space=pltpu.VMEM)] * heads,
        out_shape=[pltpu.VMEM((rows, 2 * HEAD_SIZE), jnp.bfloat16)] * heads,
        scratch_shapes=[pltpu.SemaphoreType.DMA((heads, 2))],
        compiler_params=pltpu.CompilerParams(vmem_limit_bytes=2 * MIB),
        cost_estimate=pl.CostEstimate(flops=0, bytes_accessed=2 * MIB, transcendentals=0),
    )(in_hbm(keys), in_hbm(values))


def attend(queries, marks, first, parts):
    rows = marks.shape[0] // 3
    count = len(parts)
    width = 2 * HEAD_SIZE

    def kernel(q_ref, mark_ref, *refs):
        out_ref = refs[-1]
        for i in range(count):
            left = (first + i) * width
            attend_kernel(
                q_ref.at[:, left : left + width],
                *refs[3 * i : 3 * i + 3],
                mark_ref,
                out_ref.at[:, i * width : (i + 1) * width],
            )

    flat = [in_vmem(x) for part in parts for x in part]
    return pl.pallas_call(
        kernel,
        in_specs=[pl.BlockSpec(memory_space=pltpu.VMEM)] * (2 + len(flat)),
        out_specs=pl.BlockSpec(memory_space=pltpu.VMEM),
        out_shape=pltpu.VMEM((rows, count * width), jnp.bfloat16),
        compiler_params=pltpu.CompilerParams(vmem_limit_bytes=8 * MIB),
        cost_estimate=pl.CostEstimate(
            flops=count * 4 * 1024 * 1152 * 256,
            bytes_accessed=2 * MIB,
            transcendentals=count * 1024 * 1152,
        ),
    )(queries, marks, *flat)


def project(core, own, other, own_w, other_w):
    count = len(own)
    rows = own[0].shape[0]
    depth, columns = own_w.shape
    tile = 768 if columns % 768 == 0 else 128
    tiles = columns // tile

    def kernel(core_ref, *refs):
        own_refs, other_refs = refs[:count], refs[count : 2 * count]
        own_w_ref, other_w_ref, out_ref, both, w_buf, w_sem, held, out_sem = refs[2 * count :]
        mine = pl.multiple_of(core_ref[0] * depth, depth)
        theirs = pl.multiple_of((1 - core_ref[0]) * depth, depth)

        def place(n):
            return pl.ds(pl.multiple_of(n * tile, tile), tile)

        def fetch(n):
            return [
                pltpu.make_async_copy(
                    ref.at[:, place(n)], w_buf.at[n, pl.ds(start, depth), :], w_sem.at[n, i]
                )
                for i, (ref, start) in enumerate(((own_w_ref, mine), (other_w_ref, theirs)))
            ]

        def give(n):
            return pltpu.make_async_copy(
                held.at[:, place(n)], out_ref.at[:, place(n)], out_sem.at[n]
            )

        for n in range(tiles):
            for copy in fetch(n):
                copy.start()
        for group, start in ((own_refs, mine), (other_refs, theirs)):
            at = 0
            for ref in group:
                width = ref.shape[1]
                both[:, pl.ds(pl.multiple_of(start + at, 128), width)] = ref[...]
                at += width

        @pl.loop(0, tiles)
        def _(n):
            for copy in fetch(n):
                copy.wait()
            total = jnp.dot(both[...], w_buf[n], preferred_element_type=jnp.float32)
            held[:, place(n)] = total.astype(held.dtype)
            give(n).start()

        @pl.loop(0, tiles)
        def _(n):
            give(n).wait()

    vmem = pl.BlockSpec(memory_space=pltpu.VMEM)
    hbm = pl.BlockSpec(memory_space=pltpu.HBM)
    return pl.pallas_call(
        kernel,
        in_specs=[pl.BlockSpec(memory_space=pltpu.SMEM)] + [vmem] * (2 * count) + [hbm] * 2,
        out_specs=pl.BlockSpec(memory_space=pl.ANY),
        out_shape=jax.ShapeDtypeStruct((rows, columns), jnp.bfloat16),
        scratch_shapes=[
            pltpu.VMEM((rows, 2 * depth), jnp.bfloat16),
            pltpu.VMEM((tiles, 2 * depth, tile), jnp.bfloat16),
            pltpu.SemaphoreType.DMA((tiles, 2)),
            pltpu.VMEM((rows, columns), jnp.bfloat16),
            pltpu.SemaphoreType.DMA((tiles,)),
        ],
        compiler_params=pltpu.CompilerParams(vmem_limit_bytes=40 * MIB),
        cost_estimate=pl.CostEstimate(
            flops=4 * rows * depth * columns, bytes_accessed=32 * MIB, transcendentals=0
        ),
    )(core, *[in_vmem(x) for x in own + other], in_hbm(own_w), in_hbm(other_w))


def shards(queries, keys, values, segments, out_weight):
    rows = queries.shape[0]
    heads_kv = keys.shape[1] // HEAD_SIZE
    peers = lax.axis_size("seq")
    seq_index = lax.axis_index("seq")
    core = lax.axis_index("head").astype(jnp.int32).reshape(1)
    swap = [(0, 1), (1, 0)]

    other_w = lax.ppermute(out_weight, "head", swap)
    own = pack(keys, values)
    two_on = [(i, i + 2) for i in range(peers - 2)]
    pair = [(i, i ^ 1) for i in range(peers)]
    odd = seq_index % 2 == 1
    far = [lax.ppermute(x, "seq", two_on) for x in own[:-1]]
    near = [lax.ppermute(jnp.where(odd, f, x), "seq", pair) for f, x in zip(far, own)]
    beside = lax.ppermute(own[-1], "seq", pair)
    last, far[0] = lax.optimization_barrier((jnp.concatenate([own[-1], beside]), far[0]))
    last = lax.ppermute(last, "seq", two_on)
    far.append(last[:rows])
    near.append(jnp.where(odd, beside, last[rows:]))

    halo = 2 * rows
    padded = jnp.concatenate([jnp.full((halo,), -1, jnp.int32), segments])
    seen = lax.dynamic_slice_in_dim(padded, seq_index * rows, halo + rows, 0)
    ids = lax.broadcasted_iota(jnp.int32, (halo + rows, HEAD_SIZE), 1)
    marks = in_vmem(jnp.where(seen[:, None] == ids, MARK, 0.0).astype(jnp.bfloat16))
    queries = in_vmem(queries)

    steps = [[h] for h in range(heads_kv - 2)] + [[heads_kv - 2, heads_kv - 1]]
    mine = [
        attend(queries, marks, step[0], [(own[h], near[h], far[h]) for h in step])
        for step in steps
    ]
    theirs = [lax.ppermute(x, "head", swap) for x in mine]
    return project(core, mine, theirs, out_weight, other_w)


def solution(mesh):
    placed = (
        P(("groups", "seq"), "head"),
        P(("groups", "seq"), "head"),
        P(("groups", "seq"), "head"),
        P("groups"),
        P("head", None),
    )
    return jax.shard_map(
        shards, mesh=mesh, in_specs=placed, out_specs=P(("groups", "seq"), None), check_vma=False
    )
```

```python
import jax
import jax.numpy as jnp
from jax import lax
from jax.experimental import pallas as pl
from jax.experimental.pallas import tpu as pltpu
from jax.sharding import PartitionSpec as P

HEAD_SIZE = 128
SCALAR = 168
ATTENTION_SPAN = 1024
TILE = 128
MARK = 128.0
LOG2E = 1.4426950408889634
MIB = 1 << 20


def joined(*parts):
    parts = [part for part in parts if part.shape[1]]
    return parts[0] if len(parts) == 1 else jnp.concatenate(parts, axis=1)


def attend_kernel(q_ref, own_ref, near_ref, far_ref, mark_ref, out_ref):
    rows = own_ref.shape[0]
    group = q_ref.shape[1] // HEAD_SIZE
    factor = LOG2E * SCALAR ** (-0.5)
    ones = jnp.ones((rows, HEAD_SIZE), jnp.bfloat16)

    def keys_of(ref, block):
        marks = mark_ref[block * rows : (block + 1) * rows, :]
        return jnp.concatenate([ref[:, :HEAD_SIZE], marks], axis=1)

    def values_of(ref):
        return jnp.concatenate([ref[:, HEAD_SIZE:], ones], axis=1)

    keys = [keys_of(far_ref, 0), keys_of(near_ref, 1), keys_of(own_ref, 2)]
    values = [values_of(far_ref), values_of(near_ref), values_of(own_ref)]
    row = lax.broadcasted_iota(jnp.int32, (TILE, TILE), 0)
    col = lax.broadcasted_iota(jnp.int32, (TILE, TILE), 1)
    inside = jnp.concatenate([col > row] * group, axis=0)
    causal = jnp.concatenate([col <= row] * group, axis=0)
    for t in range(rows // TILE):
        span = slice(t * TILE, (t + 1) * TILE)
        marks = mark_ref[2 * rows + t * TILE : 2 * rows + (t + 1) * TILE, :]
        query = jnp.concatenate(
            [
                jnp.concatenate([q_ref[span, g * HEAD_SIZE : (g + 1) * HEAD_SIZE], marks], axis=1)
                for g in range(group)
            ],
            axis=0,
        )
        parts = [
            (keys[0][t * TILE :], values[0][t * TILE :]),
            (keys[1], values[1]),
            (keys[2][: (t + 1) * TILE], values[2][: (t + 1) * TILE]),
        ]
        scores = [
            lax.dot_general(
                query, key, (((1,), (1,)), ((), ())), preferred_element_type=jnp.float32
            )
            for key, _ in parts
        ]
        first = jnp.where(inside, scores[0][:, :TILE], -1e30)
        scores[0] = joined(first, *([scores[0][:, TILE:]] if scores[0].shape[1] > TILE else []))
        last = jnp.where(causal, scores[2][:, t * TILE :], -1e30)
        scores[2] = joined(*([scores[2][:, : t * TILE]] if t else []), last)
        top = jnp.maximum(
            jnp.maximum(
                jnp.max(scores[0], axis=1, keepdims=True),
                jnp.max(scores[1], axis=1, keepdims=True),
            ),
            jnp.max(scores[2], axis=1, keepdims=True),
        )
        total = None
        for score, (_, value) in zip(scores, parts):
            weight = jnp.exp2((score - top) * factor).astype(jnp.bfloat16)
            term = jnp.dot(weight, value, preferred_element_type=jnp.float32)
            total = term if total is None else total + term
        result = (total[:, :HEAD_SIZE] / total[:, HEAD_SIZE:]).astype(jnp.bfloat16)
        for g in range(group):
            out_ref[span, g * HEAD_SIZE : (g + 1) * HEAD_SIZE] = result[
                g * TILE : (g + 1) * TILE
            ]


def in_vmem(x):
    return pltpu.with_memory_space_constraint(x, pltpu.VMEM)


def in_hbm(x):
    return pltpu.with_memory_space_constraint(x, pltpu.HBM)


def pack_kernel(keys_ref, values_ref, *refs):
    outs, sem = refs[:-1], refs[-1]
    copies = []
    for h, out in enumerate(outs):
        for side, ref in enumerate((keys_ref, values_ref)):
            copies.append(
                pltpu.make_async_copy(
                    ref.at[:, h * HEAD_SIZE : (h + 1) * HEAD_SIZE],
                    out.at[:, side * HEAD_SIZE : (side + 1) * HEAD_SIZE],
                    sem.at[h, side],
                )
            )
    for copy in copies:
        copy.start()
    for copy in copies:
        copy.wait()


def pack(keys, values):
    rows, heads = keys.shape[0], keys.shape[1] // HEAD_SIZE
    return pl.pallas_call(
        pack_kernel,
        in_specs=[pl.BlockSpec(memory_space=pltpu.HBM)] * 2,
        out_specs=[pl.BlockSpec(memory_space=pltpu.VMEM)] * heads,
        out_shape=[pltpu.VMEM((rows, 2 * HEAD_SIZE), jnp.bfloat16)] * heads,
        scratch_shapes=[pltpu.SemaphoreType.DMA((heads, 2))],
        compiler_params=pltpu.CompilerParams(vmem_limit_bytes=2 * MIB),
        cost_estimate=pl.CostEstimate(flops=0, bytes_accessed=2 * MIB, transcendentals=0),
    )(in_hbm(keys), in_hbm(values))


def attend(queries, marks, head, part):
    rows = marks.shape[0] // 3
    width = 2 * HEAD_SIZE

    def kernel(q_ref, mark_ref, own_ref, near_ref, far_ref, out_ref):
        left = head * width
        attend_kernel(
            q_ref.at[:, left : left + width], own_ref, near_ref, far_ref, mark_ref, out_ref
        )

    return pl.pallas_call(
        kernel,
        in_specs=[pl.BlockSpec(memory_space=pltpu.VMEM)] * 5,
        out_specs=pl.BlockSpec(memory_space=pltpu.VMEM),
        out_shape=pltpu.VMEM((rows, width), jnp.bfloat16),
        compiler_params=pltpu.CompilerParams(vmem_limit_bytes=8 * MIB),
        cost_estimate=pl.CostEstimate(
            flops=1024 * 1152, bytes_accessed=2 * MIB, transcendentals=0
        ),
    )(queries, marks, *[in_vmem(x) for x in part])


def project(core, own, other, own_w, other_w):
    count = len(own)
    rows = own[0].shape[0]
    depth, columns = own_w.shape
    tile = 768 if columns % 768 == 0 else 128
    tiles = columns // tile

    def kernel(core_ref, *refs):
        own_refs, other_refs = refs[:count], refs[count : 2 * count]
        own_w_ref, other_w_ref, out_ref, both, w_buf, w_sem, held, out_sem = refs[2 * count :]
        mine = pl.multiple_of(core_ref[0] * depth, depth)
        theirs = pl.multiple_of((1 - core_ref[0]) * depth, depth)

        def place(n):
            return pl.ds(pl.multiple_of(n * tile, tile), tile)

        def fetch(n):
            return [
                pltpu.make_async_copy(
                    ref.at[:, place(n)], w_buf.at[n, pl.ds(start, depth), :], w_sem.at[n, i]
                )
                for i, (ref, start) in enumerate(((own_w_ref, mine), (other_w_ref, theirs)))
            ]

        def give(n):
            return pltpu.make_async_copy(
                held.at[:, place(n)], out_ref.at[:, place(n)], out_sem.at[n]
            )

        for n in range(tiles):
            for copy in fetch(n):
                copy.start()
        for group, start in ((own_refs, mine), (other_refs, theirs)):
            at = 0
            for ref in group:
                width = ref.shape[1]
                both[:, pl.ds(pl.multiple_of(start + at, 128), width)] = ref[...]
                at += width

        @pl.loop(0, tiles)
        def _(n):
            for copy in fetch(n):
                copy.wait()
            total = jnp.dot(both[...], w_buf[n], preferred_element_type=jnp.float32)
            held[:, place(n)] = total.astype(held.dtype)
            give(n).start()

        @pl.loop(0, tiles)
        def _(n):
            give(n).wait()

    vmem = pl.BlockSpec(memory_space=pltpu.VMEM)
    hbm = pl.BlockSpec(memory_space=pltpu.HBM)
    return pl.pallas_call(
        kernel,
        in_specs=[pl.BlockSpec(memory_space=pltpu.SMEM)] + [vmem] * (2 * count) + [hbm] * 2,
        out_specs=pl.BlockSpec(memory_space=pl.ANY),
        out_shape=jax.ShapeDtypeStruct((rows, columns), jnp.bfloat16),
        scratch_shapes=[
            pltpu.VMEM((rows, 2 * depth), jnp.bfloat16),
            pltpu.VMEM((tiles, 2 * depth, tile), jnp.bfloat16),
            pltpu.SemaphoreType.DMA((tiles, 2)),
            pltpu.VMEM((rows, columns), jnp.bfloat16),
            pltpu.SemaphoreType.DMA((tiles,)),
        ],
        compiler_params=pltpu.CompilerParams(vmem_limit_bytes=40 * MIB),
        cost_estimate=pl.CostEstimate(
            flops=4 * rows * depth * columns, bytes_accessed=32 * MIB, transcendentals=0
        ),
    )(core, *[in_vmem(x) for x in own + other], in_hbm(own_w), in_hbm(other_w))


def shards(queries, keys, values, segments, out_weight):
    rows = queries.shape[0]
    heads_kv = keys.shape[1] // HEAD_SIZE
    peers = lax.axis_size("seq")
    seq_index = lax.axis_index("seq")
    core = lax.axis_index("head").astype(jnp.int32).reshape(1)
    swap = [(0, 1), (1, 0)]

    other_w = lax.ppermute(out_weight, "head", swap)
    own = pack(keys, values)
    two_on = [(i, i + 2) for i in range(peers - 2)]
    pair = [(i, i ^ 1) for i in range(peers)]
    odd = seq_index % 2 == 1
    far = [lax.ppermute(x, "seq", two_on) for x in own[:-1]]
    near = [lax.ppermute(jnp.where(odd, f, x), "seq", pair) for f, x in zip(far, own)]
    beside = lax.ppermute(own[-1], "seq", pair)
    last, far[0] = lax.optimization_barrier((jnp.concatenate([own[-1], beside]), far[0]))
    last = lax.ppermute(last, "seq", two_on)
    far.append(last[:rows])
    near.append(jnp.where(odd, beside, last[rows:]))

    halo = 2 * rows
    padded = jnp.concatenate([jnp.full((halo,), -1, jnp.int32), segments])
    seen = lax.dynamic_slice_in_dim(padded, seq_index * rows, halo + rows, 0)
    ids = lax.broadcasted_iota(jnp.int32, (halo + rows, HEAD_SIZE), 1)
    marks = in_vmem(jnp.where(seen[:, None] == ids, MARK, 0.0).astype(jnp.bfloat16))
    queries = in_vmem(queries)

    mine = []
    for h in range(heads_kv):
        if mine:
            marks, mine[-1] = lax.optimization_barrier((marks, mine[-1]))
        mine.append(attend(queries, marks, h, (own[h], near[h], far[h])))
    theirs = [lax.ppermute(x, "head", swap) for x in mine]
    return project(core, mine, theirs, out_weight, other_w)


def solution(mesh):
    placed = (
        P(("groups", "seq"), "head"),
        P(("groups", "seq"), "head"),
        P(("groups", "seq"), "head"),
        P("groups"),
        P("head", None),
    )
    return jax.shard_map(
        shards, mesh=mesh, in_specs=placed, out_specs=P(("groups", "seq"), None), check_vma=False
    )
```

```python
import jax
import jax.numpy as jnp
from jax import lax
from jax.experimental import pallas as pl
from jax.experimental.pallas import tpu as pltpu
from jax.sharding import PartitionSpec as P

HEAD_SIZE = 128
SCALAR = 168
ATTENTION_SPAN = 1024
TILE = 128
MARK = 128.0
LOG2E = 1.4426950408889634
MIB = 1 << 20
EARLY = 2


def joined(*parts):
    parts = [part for part in parts if part.shape[1]]
    return parts[0] if len(parts) == 1 else jnp.concatenate(parts, axis=1)


def attend_kernel(q_ref, own_ref, near_ref, far_ref, mark_ref, out_ref):
    rows = own_ref.shape[0]
    group = q_ref.shape[1] // HEAD_SIZE
    factor = LOG2E * SCALAR ** (-0.5)
    ones = jnp.ones((rows, HEAD_SIZE), jnp.bfloat16)

    def keys_of(ref, block):
        marks = mark_ref[block * rows : (block + 1) * rows, :]
        return jnp.concatenate([ref[:, :HEAD_SIZE], marks], axis=1)

    def values_of(ref):
        return jnp.concatenate([ref[:, HEAD_SIZE:], ones], axis=1)

    keys = [keys_of(far_ref, 0), keys_of(near_ref, 1), keys_of(own_ref, 2)]
    values = [values_of(far_ref), values_of(near_ref), values_of(own_ref)]
    row = lax.broadcasted_iota(jnp.int32, (TILE, TILE), 0)
    col = lax.broadcasted_iota(jnp.int32, (TILE, TILE), 1)
    inside = jnp.concatenate([col > row] * group, axis=0)
    causal = jnp.concatenate([col <= row] * group, axis=0)
    for t in range(rows // TILE):
        span = slice(t * TILE, (t + 1) * TILE)
        marks = mark_ref[2 * rows + t * TILE : 2 * rows + (t + 1) * TILE, :]
        query = jnp.concatenate(
            [
                jnp.concatenate([q_ref[span, g * HEAD_SIZE : (g + 1) * HEAD_SIZE], marks], axis=1)
                for g in range(group)
            ],
            axis=0,
        )
        parts = [
            (keys[0][t * TILE :], values[0][t * TILE :]),
            (keys[1], values[1]),
            (keys[2][: (t + 1) * TILE], values[2][: (t + 1) * TILE]),
        ]
        scores = [
            lax.dot_general(
                query, key, (((1,), (1,)), ((), ())), preferred_element_type=jnp.float32
            )
            for key, _ in parts
        ]
        first = jnp.where(inside, scores[0][:, :TILE], -1e30)
        scores[0] = joined(first, *([scores[0][:, TILE:]] if scores[0].shape[1] > TILE else []))
        last = jnp.where(causal, scores[2][:, t * TILE :], -1e30)
        scores[2] = joined(*([scores[2][:, : t * TILE]] if t else []), last)
        top = jnp.maximum(
            jnp.maximum(
                jnp.max(scores[0], axis=1, keepdims=True),
                jnp.max(scores[1], axis=1, keepdims=True),
            ),
            jnp.max(scores[2], axis=1, keepdims=True),
        )
        total = None
        for score, (_, value) in zip(scores, parts):
            weight = jnp.exp2((score - top) * factor).astype(jnp.bfloat16)
            term = jnp.dot(weight, value, preferred_element_type=jnp.float32)
            total = term if total is None else total + term
        result = (total[:, :HEAD_SIZE] / total[:, HEAD_SIZE:]).astype(jnp.bfloat16)
        for g in range(group):
            out_ref[span, g * HEAD_SIZE : (g + 1) * HEAD_SIZE] = result[
                g * TILE : (g + 1) * TILE
            ]


def in_vmem(x):
    return pltpu.with_memory_space_constraint(x, pltpu.VMEM)


def in_hbm(x):
    return pltpu.with_memory_space_constraint(x, pltpu.HBM)


def pack_kernel(keys_ref, values_ref, *refs):
    outs, sem = refs[:-1], refs[-1]
    copies = []
    for h, out in enumerate(outs):
        for side, ref in enumerate((keys_ref, values_ref)):
            copies.append(
                pltpu.make_async_copy(
                    ref.at[:, h * HEAD_SIZE : (h + 1) * HEAD_SIZE],
                    out.at[:, side * HEAD_SIZE : (side + 1) * HEAD_SIZE],
                    sem.at[h, side],
                )
            )
    for copy in copies:
        copy.start()
    for copy in copies:
        copy.wait()


def pack(keys, values):
    rows, heads = keys.shape[0], keys.shape[1] // HEAD_SIZE
    return pl.pallas_call(
        pack_kernel,
        in_specs=[pl.BlockSpec(memory_space=pltpu.HBM)] * 2,
        out_specs=[pl.BlockSpec(memory_space=pltpu.VMEM)] * heads,
        out_shape=[pltpu.VMEM((rows, 2 * HEAD_SIZE), jnp.bfloat16)] * heads,
        scratch_shapes=[pltpu.SemaphoreType.DMA((heads, 2))],
        compiler_params=pltpu.CompilerParams(vmem_limit_bytes=2 * MIB),
        cost_estimate=pl.CostEstimate(flops=0, bytes_accessed=2 * MIB, transcendentals=0),
    )(in_hbm(keys), in_hbm(values))


def prepare(seq_index, segments, queries):
    rows = queries.shape[0]
    slab = segments.shape[0]
    blocks = 3

    def kernel(index_ref, seg_ref, q_ref, mark_ref, q_out, sem):
        copy = pltpu.make_async_copy(q_ref, q_out, sem)
        copy.start()
        ids = lax.broadcasted_iota(jnp.int32, (HEAD_SIZE, rows), 0)
        for b in range(blocks):
            block = index_ref[0] + b - (blocks - 1)
            seen = seg_ref[pl.ds(jnp.maximum(block, 0), 1), :]
            hit = (seen == ids) & (block >= 0)
            mark = jnp.where(hit, MARK, 0.0)
            mark_ref[b * rows : (b + 1) * rows, :] = mark.T.astype(jnp.bfloat16)
        copy.wait()

    vmem = pl.BlockSpec(memory_space=pltpu.VMEM)
    return pl.pallas_call(
        kernel,
        in_specs=[
            pl.BlockSpec(memory_space=pltpu.SMEM),
            vmem,
            pl.BlockSpec(memory_space=pltpu.HBM),
        ],
        out_specs=[vmem, vmem],
        out_shape=[
            pltpu.VMEM((blocks * rows, HEAD_SIZE), jnp.bfloat16),
            pltpu.VMEM(queries.shape, queries.dtype),
        ],
        scratch_shapes=[pltpu.SemaphoreType.DMA],
        compiler_params=pltpu.CompilerParams(vmem_limit_bytes=4 * MIB),
        cost_estimate=pl.CostEstimate(flops=1024, bytes_accessed=1024, transcendentals=0),
    )(seq_index, segments.reshape(slab // rows, rows), in_hbm(queries))


def column_tile(columns):
    return 768 if columns % 768 == 0 else 128


def tile_copy(weights, n, into, sem):
    tile = into.shape[1]
    place = pl.ds(pl.multiple_of(n * tile, tile), tile)
    return pltpu.make_async_copy(weights.at[:, place], into, sem)


def attend(queries, marks, head, part, weights=None):
    rows = marks.shape[0] // 3
    width = 2 * HEAD_SIZE

    def kernel(q_ref, mark_ref, own_ref, near_ref, far_ref, *refs):
        if weights is None:
            (out_ref,) = refs
        else:
            w_ref, out_ref, *tile_refs, sem = refs
            copies = [tile_copy(w_ref, n, ref, sem.at[n]) for n, ref in enumerate(tile_refs)]
            for copy in copies:
                copy.start()
        left = head * width
        attend_kernel(
            q_ref.at[:, left : left + width], own_ref, near_ref, far_ref, mark_ref, out_ref
        )
        if weights is not None:
            for copy in copies:
                copy.wait()

    vmem = pl.BlockSpec(memory_space=pltpu.VMEM)
    specs, outs = [vmem] * 5, [pltpu.VMEM((rows, width), jnp.bfloat16)]
    flat, scratch = [], []
    if weights is not None:
        depth, columns = weights.shape
        specs.append(pl.BlockSpec(memory_space=pltpu.HBM))
        flat.append(in_hbm(weights))
        outs += [pltpu.VMEM((depth, column_tile(columns)), jnp.bfloat16)] * EARLY
        scratch.append(pltpu.SemaphoreType.DMA((EARLY,)))
    return pl.pallas_call(
        kernel,
        in_specs=specs,
        out_specs=[vmem] * len(outs),
        out_shape=outs,
        scratch_shapes=scratch,
        compiler_params=pltpu.CompilerParams(vmem_limit_bytes=8 * MIB),
        cost_estimate=pl.CostEstimate(flops=1024, bytes_accessed=1024, transcendentals=0),
    )(queries, marks, *[in_vmem(x) for x in part], *flat)


def project(own, other, own_w, other_w, ready):
    count = len(own)
    rows = own[0].shape[0]
    depth, columns = own_w.shape
    tile = column_tile(columns)
    tiles = columns // tile
    late = tiles - len(ready)

    def kernel(*refs):
        own_refs, other_refs = refs[:count], refs[count : 2 * count]
        own_w_ref, other_w_ref, *refs = refs[2 * count :]
        ready_refs, refs = refs[: len(ready)], refs[len(ready) :]
        out_ref, row, other_row, held, out_sem, w_buf, w_sem = refs

        def place(n):
            return pl.ds(pl.multiple_of(n * tile, tile), tile)

        def give(n):
            return pltpu.make_async_copy(
                held.at[:, place(n)], out_ref.at[:, place(n)], out_sem.at[n]
            )

        def coming(n):
            slot = n - len(ready)
            return tile_copy(other_w_ref, n, w_buf.at[slot], w_sem.at[slot])

        def multiply(n, weight):
            term = jnp.dot(row[...], own_w_ref[:, place(n)], preferred_element_type=jnp.float32)
            other_term = jnp.dot(
                other_row[...], weight[...], preferred_element_type=jnp.float32
            )
            held[:, place(n)] = (term + other_term).astype(held.dtype)
            give(n).start()

        for n in range(len(ready), tiles):
            coming(n).start()
        for into, group in ((row, own_refs), (other_row, other_refs)):
            for i, ref in enumerate(group):
                width = ref.shape[1]
                into[:, i * width : (i + 1) * width] = ref[...]
        for n, ref in enumerate(ready_refs):
            multiply(n, ref)

        @pl.loop(len(ready), tiles)
        def _(n):
            coming(n).wait()
            multiply(n, w_buf.at[n - len(ready)])

        @pl.loop(0, tiles)
        def _(n):
            give(n).wait()

    vmem = pl.BlockSpec(memory_space=pltpu.VMEM)
    hbm = pl.BlockSpec(memory_space=pltpu.HBM)
    return pl.pallas_call(
        kernel,
        in_specs=[vmem] * (2 * count + 1) + [hbm] + [vmem] * len(ready),
        out_specs=pl.BlockSpec(memory_space=pl.ANY),
        out_shape=jax.ShapeDtypeStruct((rows, columns), jnp.bfloat16),
        scratch_shapes=[
            pltpu.VMEM((rows, depth), jnp.bfloat16),
            pltpu.VMEM((rows, depth), jnp.bfloat16),
            pltpu.VMEM((rows, columns), jnp.bfloat16),
            pltpu.SemaphoreType.DMA((tiles,)),
            pltpu.VMEM((late, depth, tile), jnp.bfloat16),
            pltpu.SemaphoreType.DMA((late,)),
        ],
        compiler_params=pltpu.CompilerParams(vmem_limit_bytes=24 * MIB),
        cost_estimate=pl.CostEstimate(
            flops=4 * rows * depth * columns, bytes_accessed=32 * MIB, transcendentals=0
        ),
    )(*[in_vmem(x) for x in own + other], in_vmem(own_w), in_hbm(other_w), *ready)


def shards(queries, keys, values, segments, out_weight):
    rows = queries.shape[0]
    heads_kv = keys.shape[1] // HEAD_SIZE
    peers = lax.axis_size("seq")
    seq_index = lax.axis_index("seq")
    swap = [(0, 1), (1, 0)]

    own = list(pack(keys, values))
    out_weight, own[0] = lax.optimization_barrier((out_weight, own[0]))
    other_w = lax.ppermute(out_weight, "head", swap)
    two_on = [(i, i + 2) for i in range(peers - 2)]
    pair = [(i, i ^ 1) for i in range(peers)]
    odd = seq_index % 2 == 1
    far = [lax.ppermute(x, "seq", two_on) for x in own[:-1]]
    queries, far[0] = lax.optimization_barrier((queries, far[0]))
    marks, queries = prepare(seq_index.astype(jnp.int32).reshape(1), segments, queries)
    far[1], marks = lax.optimization_barrier((far[1], marks))
    near = [lax.ppermute(jnp.where(odd, f, x), "seq", pair) for f, x in zip(far, own)]
    beside = lax.ppermute(own[-1], "seq", pair)
    last, far[0] = lax.optimization_barrier((jnp.concatenate([own[-1], beside]), far[0]))
    last = lax.ppermute(last, "seq", two_on)
    far.append(last[:rows])
    near.append(jnp.where(odd, beside, last[rows:]))

    mine, ready = [], []
    for h in range(heads_kv):
        if mine:
            marks, mine[-1] = lax.optimization_barrier((marks, mine[-1]))
        weights = other_w if h == heads_kv - 1 else None
        result, *tile = attend(queries, marks, h, (own[h], near[h], far[h]), weights)
        mine.append(result)
        ready += tile
    theirs = [lax.ppermute(x, "head", swap) for x in mine]
    return project(mine, theirs, out_weight, other_w, ready)


def solution(mesh):
    placed = (
        P(("groups", "seq"), "head"),
        P(("groups", "seq"), "head"),
        P(("groups", "seq"), "head"),
        P("groups"),
        P("head", None),
    )
    return jax.shard_map(
        shards, mesh=mesh, in_specs=placed, out_specs=P(("groups", "seq"), None), check_vma=False
    )
```

```python
import jax
import jax.numpy as jnp
from jax import lax
from jax.experimental import pallas as pl
from jax.experimental.pallas import tpu as pltpu
from jax.sharding import PartitionSpec as P

HEAD_SIZE = 128
SCALAR = 168
ATTENTION_SPAN = 1024
TILE = 128
MARK = 128.0
LOG2E = 1.4426950408889634
MIB = 1 << 20
EARLY = 2


def joined(*parts):
    parts = [part for part in parts if part.shape[1]]
    return parts[0] if len(parts) == 1 else jnp.concatenate(parts, axis=1)


def attend_kernel(q_ref, own_ref, near_ref, far_ref, mark_ref, out_ref):
    rows = own_ref.shape[0]
    group = q_ref.shape[1] // HEAD_SIZE
    factor = LOG2E * SCALAR ** (-0.5)
    ones = jnp.ones((rows, HEAD_SIZE), jnp.bfloat16)

    def keys_of(ref, block):
        marks = mark_ref[block * rows : (block + 1) * rows, :]
        return jnp.concatenate([ref[:, :HEAD_SIZE], marks], axis=1)

    def values_of(ref):
        return jnp.concatenate([ref[:, HEAD_SIZE:], ones], axis=1)

    keys = [keys_of(far_ref, 0), keys_of(near_ref, 1), keys_of(own_ref, 2)]
    values = [values_of(far_ref), values_of(near_ref), values_of(own_ref)]
    row = lax.broadcasted_iota(jnp.int32, (TILE, TILE), 0)
    col = lax.broadcasted_iota(jnp.int32, (TILE, TILE), 1)
    inside = jnp.concatenate([col > row] * group, axis=0)
    causal = jnp.concatenate([col <= row] * group, axis=0)
    for t in range(rows // TILE):
        span = slice(t * TILE, (t + 1) * TILE)
        marks = mark_ref[2 * rows + t * TILE : 2 * rows + (t + 1) * TILE, :]
        query = jnp.concatenate(
            [
                jnp.concatenate([q_ref[span, g * HEAD_SIZE : (g + 1) * HEAD_SIZE], marks], axis=1)
                for g in range(group)
            ],
            axis=0,
        )
        parts = [
            (keys[0][t * TILE :], values[0][t * TILE :]),
            (keys[1], values[1]),
            (keys[2][: (t + 1) * TILE], values[2][: (t + 1) * TILE]),
        ]
        scores = [
            lax.dot_general(
                query, key, (((1,), (1,)), ((), ())), preferred_element_type=jnp.float32
            )
            for key, _ in parts
        ]
        first = jnp.where(inside, scores[0][:, :TILE], -1e30)
        scores[0] = joined(first, *([scores[0][:, TILE:]] if scores[0].shape[1] > TILE else []))
        last = jnp.where(causal, scores[2][:, t * TILE :], -1e30)
        scores[2] = joined(*([scores[2][:, : t * TILE]] if t else []), last)
        top = jnp.maximum(
            jnp.maximum(
                jnp.max(scores[0], axis=1, keepdims=True),
                jnp.max(scores[1], axis=1, keepdims=True),
            ),
            jnp.max(scores[2], axis=1, keepdims=True),
        )
        total = None
        for score, (_, value) in zip(scores, parts):
            weight = jnp.exp2((score - top) * factor).astype(jnp.bfloat16)
            term = jnp.dot(weight, value, preferred_element_type=jnp.float32)
            total = term if total is None else total + term
        result = (total[:, :HEAD_SIZE] / total[:, HEAD_SIZE:]).astype(jnp.bfloat16)
        for g in range(group):
            out_ref[span, g * HEAD_SIZE : (g + 1) * HEAD_SIZE] = result[
                g * TILE : (g + 1) * TILE
            ]


def in_vmem(x):
    return pltpu.with_memory_space_constraint(x, pltpu.VMEM)


def in_hbm(x):
    return pltpu.with_memory_space_constraint(x, pltpu.HBM)


def pack_kernel(keys_ref, values_ref, *refs):
    outs, sem = refs[:-1], refs[-1]
    copies = []
    for h, out in enumerate(outs):
        for side, ref in enumerate((keys_ref, values_ref)):
            copies.append(
                pltpu.make_async_copy(
                    ref.at[:, h * HEAD_SIZE : (h + 1) * HEAD_SIZE],
                    out.at[:, side * HEAD_SIZE : (side + 1) * HEAD_SIZE],
                    sem.at[h, side],
                )
            )
    for copy in copies:
        copy.start()
    for copy in copies:
        copy.wait()


def pack(keys, values):
    rows, heads = keys.shape[0], keys.shape[1] // HEAD_SIZE
    return pl.pallas_call(
        pack_kernel,
        in_specs=[pl.BlockSpec(memory_space=pltpu.HBM)] * 2,
        out_specs=[pl.BlockSpec(memory_space=pltpu.VMEM)] * heads,
        out_shape=[pltpu.VMEM((rows, 2 * HEAD_SIZE), jnp.bfloat16)] * heads,
        scratch_shapes=[pltpu.SemaphoreType.DMA((heads, 2))],
        compiler_params=pltpu.CompilerParams(vmem_limit_bytes=2 * MIB),
        cost_estimate=pl.CostEstimate(flops=0, bytes_accessed=2 * MIB, transcendentals=0),
    )(in_hbm(keys), in_hbm(values))


def prepare(seq_index, segments, queries):
    rows = queries.shape[0]
    slab = segments.shape[0]
    blocks = 3

    def kernel(index_ref, seg_ref, q_ref, mark_ref, q_out, sem):
        copy = pltpu.make_async_copy(q_ref, q_out, sem)
        copy.start()
        ids = lax.broadcasted_iota(jnp.int32, (HEAD_SIZE, rows), 0)
        for b in range(blocks):
            block = index_ref[0] + b - (blocks - 1)
            seen = seg_ref[pl.ds(jnp.maximum(block, 0), 1), :]
            hit = (seen == ids) & (block >= 0)
            mark = jnp.where(hit, MARK, 0.0)
            mark_ref[b * rows : (b + 1) * rows, :] = mark.T.astype(jnp.bfloat16)
        copy.wait()

    vmem = pl.BlockSpec(memory_space=pltpu.VMEM)
    return pl.pallas_call(
        kernel,
        in_specs=[
            pl.BlockSpec(memory_space=pltpu.SMEM),
            vmem,
            pl.BlockSpec(memory_space=pltpu.HBM),
        ],
        out_specs=[vmem, vmem],
        out_shape=[
            pltpu.VMEM((blocks * rows, HEAD_SIZE), jnp.bfloat16),
            pltpu.VMEM(queries.shape, queries.dtype),
        ],
        scratch_shapes=[pltpu.SemaphoreType.DMA],
        compiler_params=pltpu.CompilerParams(vmem_limit_bytes=4 * MIB),
        cost_estimate=pl.CostEstimate(flops=1024, bytes_accessed=1024, transcendentals=0),
    )(seq_index, segments.reshape(slab // rows, rows), in_hbm(queries))


def column_tile(columns):
    return 768 if columns % 768 == 0 else 128


def tile_copy(weights, n, into, sem):
    tile = into.shape[1]
    place = pl.ds(pl.multiple_of(n * tile, tile), tile)
    return pltpu.make_async_copy(weights.at[:, place], into, sem)


def attend(queries, marks, head, part, weights=None):
    rows = marks.shape[0] // 3
    width = 2 * HEAD_SIZE

    def kernel(q_ref, mark_ref, own_ref, near_ref, far_ref, *refs):
        if weights is None:
            (out_ref,) = refs
        else:
            w_ref, out_ref, *tile_refs, sem = refs
            copies = [tile_copy(w_ref, n, ref, sem.at[n]) for n, ref in enumerate(tile_refs)]
            for copy in copies:
                copy.start()
        left = head * width
        attend_kernel(
            q_ref.at[:, left : left + width], own_ref, near_ref, far_ref, mark_ref, out_ref
        )
        if weights is not None:
            for copy in copies:
                copy.wait()

    vmem = pl.BlockSpec(memory_space=pltpu.VMEM)
    specs, outs = [vmem] * 5, [pltpu.VMEM((rows, width), jnp.bfloat16)]
    flat, scratch = [], []
    if weights is not None:
        depth, columns = weights.shape
        specs.append(pl.BlockSpec(memory_space=pltpu.HBM))
        flat.append(in_hbm(weights))
        outs += [pltpu.VMEM((depth, column_tile(columns)), jnp.bfloat16)] * EARLY
        scratch.append(pltpu.SemaphoreType.DMA((EARLY,)))
    return pl.pallas_call(
        kernel,
        in_specs=specs,
        out_specs=[vmem] * len(outs),
        out_shape=outs,
        scratch_shapes=scratch,
        compiler_params=pltpu.CompilerParams(vmem_limit_bytes=8 * MIB),
        cost_estimate=pl.CostEstimate(flops=1024, bytes_accessed=1024, transcendentals=0),
    )(queries, marks, *[in_vmem(x) for x in part], *flat)


def project_early(own, other, own_w, ready):
    count = len(own)
    rows, width = own[0].shape
    tile = ready.shape[1]
    depth = count * width

    def kernel(*refs):
        own_refs, other_refs = refs[:count], refs[count : 2 * count]
        own_w_ref, ready_ref, out_ref, row, other_row = refs[2 * count :]
        for into, group in ((row, own_refs), (other_row, other_refs)):
            for i, ref in enumerate(group):
                into[:, i * width : (i + 1) * width] = ref[...]
        term = jnp.dot(row[...], own_w_ref[:depth, :tile], preferred_element_type=jnp.float32)
        other_term = jnp.dot(
            other_row[...], ready_ref[:depth, :], preferred_element_type=jnp.float32
        )
        out_ref[...] = term + other_term

    vmem = pl.BlockSpec(memory_space=pltpu.VMEM)
    return pl.pallas_call(
        kernel,
        in_specs=[vmem] * (2 * count + 2),
        out_specs=vmem,
        out_shape=pltpu.VMEM((rows, tile), jnp.float32),
        scratch_shapes=[pltpu.VMEM((rows, depth), jnp.bfloat16)] * 2,
        compiler_params=pltpu.CompilerParams(vmem_limit_bytes=8 * MIB),
        cost_estimate=pl.CostEstimate(
            flops=4 * rows * depth * tile, bytes_accessed=4 * MIB, transcendentals=0
        ),
    )(*[in_vmem(x) for x in own + other], in_vmem(own_w), ready)


def project(own, other, own_w, other_w, ready, base):
    count = len(own)
    rows = own[0].shape[0]
    depth, columns = own_w.shape
    tile = column_tile(columns)
    tiles = columns // tile
    late = tiles - len(ready)

    def kernel(*refs):
        own_refs, other_refs = refs[:count], refs[count : 2 * count]
        own_w_ref, other_w_ref, *refs = refs[2 * count :]
        base_ref, *refs = refs
        ready_refs, refs = refs[: len(ready)], refs[len(ready) :]
        out_ref, row, other_row, held, out_sem, w_buf, w_sem = refs

        def place(n):
            return pl.ds(pl.multiple_of(n * tile, tile), tile)

        def give(n):
            return pltpu.make_async_copy(
                held.at[:, place(n)], out_ref.at[:, place(n)], out_sem.at[n]
            )

        def coming(n):
            slot = n - len(ready)
            return tile_copy(other_w_ref, n, w_buf.at[slot], w_sem.at[slot])

        def multiply(n, weight, base=None):
            down = slice(0 if base is None else depth - own_refs[-1].shape[1], depth)
            term = jnp.dot(
                row[:, down], own_w_ref[down, place(n)], preferred_element_type=jnp.float32
            )
            other_term = jnp.dot(
                other_row[:, down], weight[down, :], preferred_element_type=jnp.float32
            )
            total = term + other_term
            if base is not None:
                total = total + base[...]
            held[:, place(n)] = total.astype(held.dtype)
            give(n).start()

        for n in range(len(ready), tiles):
            coming(n).start()
        for into, group in ((row, own_refs), (other_row, other_refs)):
            for i, ref in enumerate(group):
                width = ref.shape[1]
                into[:, i * width : (i + 1) * width] = ref[...]
        for n, ref in enumerate(ready_refs):
            multiply(n, ref, base_ref if n == 0 else None)

        @pl.loop(len(ready), tiles)
        def _(n):
            coming(n).wait()
            multiply(n, w_buf.at[n - len(ready)])

        @pl.loop(0, tiles)
        def _(n):
            give(n).wait()

    vmem = pl.BlockSpec(memory_space=pltpu.VMEM)
    hbm = pl.BlockSpec(memory_space=pltpu.HBM)
    return pl.pallas_call(
        kernel,
        in_specs=[vmem] * (2 * count + 1) + [hbm] + [vmem] * (1 + len(ready)),
        out_specs=pl.BlockSpec(memory_space=pl.ANY),
        out_shape=jax.ShapeDtypeStruct((rows, columns), jnp.bfloat16),
        scratch_shapes=[
            pltpu.VMEM((rows, depth), jnp.bfloat16),
            pltpu.VMEM((rows, depth), jnp.bfloat16),
            pltpu.VMEM((rows, columns), jnp.bfloat16),
            pltpu.SemaphoreType.DMA((tiles,)),
            pltpu.VMEM((late, depth, tile), jnp.bfloat16),
            pltpu.SemaphoreType.DMA((late,)),
        ],
        compiler_params=pltpu.CompilerParams(vmem_limit_bytes=24 * MIB),
        cost_estimate=pl.CostEstimate(
            flops=4 * rows * depth * columns, bytes_accessed=32 * MIB, transcendentals=0
        ),
    )(*[in_vmem(x) for x in own + other], in_vmem(own_w), in_hbm(other_w), base, *ready)


def shards(queries, keys, values, segments, out_weight):
    rows = queries.shape[0]
    heads_kv = keys.shape[1] // HEAD_SIZE
    peers = lax.axis_size("seq")
    seq_index = lax.axis_index("seq")
    swap = [(0, 1), (1, 0)]

    own = list(pack(keys, values))
    out_weight, own[0] = lax.optimization_barrier((out_weight, own[0]))
    other_w = lax.ppermute(out_weight, "head", swap)
    two_on = [(i, i + 2) for i in range(peers - 2)]
    pair = [(i, i ^ 1) for i in range(peers)]
    odd = seq_index % 2 == 1
    far = [lax.ppermute(x, "seq", two_on) for x in own[:-1]]
    queries, far[0] = lax.optimization_barrier((queries, far[0]))
    marks, queries = prepare(seq_index.astype(jnp.int32).reshape(1), segments, queries)
    far[1], marks = lax.optimization_barrier((far[1], marks))
    near = [lax.ppermute(jnp.where(odd, f, x), "seq", pair) for f, x in zip(far, own)]
    beside = lax.ppermute(own[-1], "seq", pair)
    last, far[0] = lax.optimization_barrier((jnp.concatenate([own[-1], beside]), far[0]))
    last = lax.ppermute(last, "seq", two_on)
    far.append(last[:rows])
    near.append(jnp.where(odd, beside, last[rows:]))

    mine, ready = [], []
    for h in range(heads_kv):
        if mine:
            marks, mine[-1] = lax.optimization_barrier((marks, mine[-1]))
        weights = other_w if h == heads_kv - 1 else None
        result, *tile = attend(queries, marks, h, (own[h], near[h], far[h]), weights)
        mine.append(result)
        ready += tile
    theirs = [lax.ppermute(x, "head", swap) for x in mine]
    base = project_early(mine[:-1], theirs[:-1], out_weight, ready[0])
    return project(mine, theirs, out_weight, other_w, ready, base)


def solution(mesh):
    placed = (
        P(("groups", "seq"), "head"),
        P(("groups", "seq"), "head"),
        P(("groups", "seq"), "head"),
        P("groups"),
        P("head", None),
    )
    return jax.shard_map(
        shards, mesh=mesh, in_specs=placed, out_specs=P(("groups", "seq"), None), check_vma=False
    )
```

```python
import functools

import jax
import jax.numpy as jnp
from jax import lax
from jax.experimental import pallas as pl
from jax.experimental.pallas import tpu as pltpu
from jax.sharding import PartitionSpec as P

HEAD_SIZE = 128
SCALAR = 168
ATTENTION_SPAN = 1024
TILE = 128
MARK = 128.0
LOG2E = 1.4426950408889634
MIB = 1 << 20
EARLY = 2


def joined(*parts):
    parts = [part for part in parts if part.shape[1]]
    return parts[0] if len(parts) == 1 else jnp.concatenate(parts, axis=1)


def attend_kernel(q_ref, own_ref, near_ref, far_ref, mark_ref, out_ref):
    rows = own_ref.shape[0]
    group = q_ref.shape[1] // HEAD_SIZE
    factor = LOG2E * SCALAR ** (-0.5)
    ones = jnp.ones((rows, HEAD_SIZE), jnp.bfloat16)

    def keys_of(ref, block):
        marks = mark_ref[block * rows : (block + 1) * rows, :]
        return jnp.concatenate([ref[:, :HEAD_SIZE], marks], axis=1)

    def values_of(ref):
        return jnp.concatenate([ref[:, HEAD_SIZE:], ones], axis=1)

    keys = [keys_of(far_ref, 0), keys_of(near_ref, 1), keys_of(own_ref, 2)]
    values = [values_of(far_ref), values_of(near_ref), values_of(own_ref)]
    row = lax.broadcasted_iota(jnp.int32, (TILE, TILE), 0)
    col = lax.broadcasted_iota(jnp.int32, (TILE, TILE), 1)
    inside = jnp.concatenate([col > row] * group, axis=0)
    causal = jnp.concatenate([col <= row] * group, axis=0)

    def score_tile(t):
        span = slice(t * TILE, (t + 1) * TILE)
        marks = mark_ref[2 * rows + t * TILE : 2 * rows + (t + 1) * TILE, :]
        query = jnp.concatenate(
            [
                jnp.concatenate([q_ref[span, g * HEAD_SIZE : (g + 1) * HEAD_SIZE], marks], axis=1)
                for g in range(group)
            ],
            axis=0,
        )
        parts = [keys[0][t * TILE :], keys[1], keys[2][: (t + 1) * TILE]]
        scores = [
            lax.dot_general(
                query, key, (((1,), (1,)), ((), ())), preferred_element_type=jnp.float32
            )
            for key in parts
        ]
        first = jnp.where(inside, scores[0][:, :TILE], -1e30)
        scores[0] = joined(first, *([scores[0][:, TILE:]] if scores[0].shape[1] > TILE else []))
        last = jnp.where(causal, scores[2][:, t * TILE :], -1e30)
        scores[2] = joined(*([scores[2][:, : t * TILE]] if t else []), last)
        return scores

    def weigh_tile(t, scores):
        columns = [
            score[:, c : c + HEAD_SIZE]
            for score in scores
            for c in range(0, score.shape[1], HEAD_SIZE)
        ]
        top = jnp.max(functools.reduce(jnp.maximum, columns), axis=1, keepdims=True)
        return [jnp.exp2((score - top) * factor).astype(jnp.bfloat16) for score in scores]

    def give_tile(t, weights):
        span = slice(t * TILE, (t + 1) * TILE)
        parts = [values[0][t * TILE :], values[1], values[2][: (t + 1) * TILE]]
        total = None
        for weight, value in zip(weights, parts):
            term = jnp.dot(weight, value, preferred_element_type=jnp.float32)
            total = term if total is None else total + term
        result = (total[:, :HEAD_SIZE] / total[:, HEAD_SIZE:]).astype(jnp.bfloat16)
        for g in range(group):
            out_ref[span, g * HEAD_SIZE : (g + 1) * HEAD_SIZE] = result[
                g * TILE : (g + 1) * TILE
            ]

    tiles = rows // TILE
    scores = [score_tile(t) for t in range(tiles)]
    weights = [weigh_tile(t, scores[t]) for t in range(tiles)]
    for t in range(tiles):
        give_tile(t, weights[t])


def in_vmem(x):
    return pltpu.with_memory_space_constraint(x, pltpu.VMEM)


def in_hbm(x):
    return pltpu.with_memory_space_constraint(x, pltpu.HBM)


def pack_kernel(keys_ref, values_ref, *refs):
    outs, sem = refs[:-1], refs[-1]
    copies = []
    for h, out in enumerate(outs):
        for side, ref in enumerate((keys_ref, values_ref)):
            copies.append(
                pltpu.make_async_copy(
                    ref.at[:, h * HEAD_SIZE : (h + 1) * HEAD_SIZE],
                    out.at[:, side * HEAD_SIZE : (side + 1) * HEAD_SIZE],
                    sem.at[h, side],
                )
            )
    for copy in copies:
        copy.start()
    for copy in copies:
        copy.wait()


def pack(keys, values):
    rows, heads = keys.shape[0], keys.shape[1] // HEAD_SIZE
    return pl.pallas_call(
        pack_kernel,
        in_specs=[pl.BlockSpec(memory_space=pltpu.HBM)] * 2,
        out_specs=[pl.BlockSpec(memory_space=pltpu.VMEM)] * heads,
        out_shape=[pltpu.VMEM((rows, 2 * HEAD_SIZE), jnp.bfloat16)] * heads,
        scratch_shapes=[pltpu.SemaphoreType.DMA((heads, 2))],
        compiler_params=pltpu.CompilerParams(vmem_limit_bytes=2 * MIB),
        cost_estimate=pl.CostEstimate(flops=0, bytes_accessed=2 * MIB, transcendentals=0),
    )(in_hbm(keys), in_hbm(values))


def prepare(seq_index, segments, queries):
    rows = queries.shape[0]
    slab = segments.shape[0]
    blocks = 3

    def kernel(index_ref, seg_ref, q_ref, mark_ref, q_out, sem):
        copy = pltpu.make_async_copy(q_ref, q_out, sem)
        copy.start()
        ids = lax.broadcasted_iota(jnp.int32, (HEAD_SIZE, rows), 0)
        for b in range(blocks):
            block = index_ref[0] + b - (blocks - 1)
            seen = seg_ref[pl.ds(jnp.maximum(block, 0), 1), :]
            hit = (seen == ids) & (block >= 0)
            mark = jnp.where(hit, MARK, 0.0)
            mark_ref[b * rows : (b + 1) * rows, :] = mark.T.astype(jnp.bfloat16)
        copy.wait()

    vmem = pl.BlockSpec(memory_space=pltpu.VMEM)
    return pl.pallas_call(
        kernel,
        in_specs=[
            pl.BlockSpec(memory_space=pltpu.SMEM),
            vmem,
            pl.BlockSpec(memory_space=pltpu.HBM),
        ],
        out_specs=[vmem, vmem],
        out_shape=[
            pltpu.VMEM((blocks * rows, HEAD_SIZE), jnp.bfloat16),
            pltpu.VMEM(queries.shape, queries.dtype),
        ],
        scratch_shapes=[pltpu.SemaphoreType.DMA],
        compiler_params=pltpu.CompilerParams(vmem_limit_bytes=4 * MIB),
        cost_estimate=pl.CostEstimate(flops=1024, bytes_accessed=1024, transcendentals=0),
    )(seq_index, segments.reshape(slab // rows, rows), in_hbm(queries))


def column_tile(columns):
    return 768 if columns % 768 == 0 else 128


def tile_copy(weights, n, into, sem):
    tile = into.shape[1]
    place = pl.ds(pl.multiple_of(n * tile, tile), tile)
    return pltpu.make_async_copy(weights.at[:, place], into, sem)


def attend(queries, marks, head, part, weights=None):
    rows = marks.shape[0] // 3
    width = 2 * HEAD_SIZE

    def kernel(q_ref, mark_ref, own_ref, near_ref, far_ref, *refs):
        if weights is None:
            (out_ref,) = refs
        else:
            w_ref, out_ref, *tile_refs, sem = refs
            copies = [tile_copy(w_ref, n, ref, sem.at[n]) for n, ref in enumerate(tile_refs)]
            for copy in copies:
                copy.start()
        left = head * width
        attend_kernel(
            q_ref.at[:, left : left + width], own_ref, near_ref, far_ref, mark_ref, out_ref
        )
        if weights is not None:
            for copy in copies:
                copy.wait()

    vmem = pl.BlockSpec(memory_space=pltpu.VMEM)
    specs, outs = [vmem] * 5, [pltpu.VMEM((rows, width), jnp.bfloat16)]
    flat, scratch = [], []
    if weights is not None:
        depth, columns = weights.shape
        specs.append(pl.BlockSpec(memory_space=pltpu.HBM))
        flat.append(in_hbm(weights))
        outs += [pltpu.VMEM((depth, column_tile(columns)), jnp.bfloat16)] * EARLY
        scratch.append(pltpu.SemaphoreType.DMA((EARLY,)))
    return pl.pallas_call(
        kernel,
        in_specs=specs,
        out_specs=[vmem] * len(outs),
        out_shape=outs,
        scratch_shapes=scratch,
        compiler_params=pltpu.CompilerParams(vmem_limit_bytes=8 * MIB),
        cost_estimate=pl.CostEstimate(flops=1024, bytes_accessed=1024, transcendentals=0),
    )(queries, marks, *[in_vmem(x) for x in part], *flat)


def stage_kernel(in_ref, out_ref, sem, *, skip):
    rows, columns = out_ref.shape
    copy = pltpu.make_async_copy(in_ref.at[:rows, skip : skip + columns], out_ref, sem)
    copy.start()
    copy.wait()


def stage(own_w):
    depth, columns = own_w.shape
    skip = column_tile(columns)
    return pl.pallas_call(
        functools.partial(stage_kernel, skip=skip),
        in_specs=[pl.BlockSpec(memory_space=pltpu.HBM)],
        out_specs=pl.BlockSpec(memory_space=pltpu.VMEM),
        out_shape=pltpu.VMEM((depth // 2, columns - skip), own_w.dtype),
        scratch_shapes=[pltpu.SemaphoreType.DMA],
        compiler_params=pltpu.CompilerParams(vmem_limit_bytes=MIB),
        cost_estimate=pl.CostEstimate(flops=1024, bytes_accessed=1024, transcendentals=0),
    )(in_hbm(own_w))


def project_own(own, upper_w, tile):
    count = len(own)
    rows, width = own[0].shape
    columns = upper_w.shape[1]
    depth = count * width

    def kernel(*refs):
        own_refs, (upper_w_ref, out_ref, row) = refs[:count], refs[count:]
        for i, ref in enumerate(own_refs):
            row[:, i * width : (i + 1) * width] = ref[...]

        @pl.loop(0, columns // tile)
        def _(n):
            place = pl.ds(pl.multiple_of(n * tile, tile), tile)
            out_ref[:, place] = jnp.dot(
                row[...], upper_w_ref[:, place], preferred_element_type=jnp.float32
            )

    vmem = pl.BlockSpec(memory_space=pltpu.VMEM)
    return pl.pallas_call(
        kernel,
        in_specs=[vmem] * (count + 1),
        out_specs=vmem,
        out_shape=pltpu.VMEM((rows, columns), jnp.float32),
        scratch_shapes=[pltpu.VMEM((rows, depth), jnp.bfloat16)],
        compiler_params=pltpu.CompilerParams(vmem_limit_bytes=6 * MIB),
        cost_estimate=pl.CostEstimate(flops=1024, bytes_accessed=1024, transcendentals=0),
    )(*[in_vmem(x) for x in own], upper_w)


def project_early(own, other, own_w, ready):
    count = len(own)
    rows, width = own[0].shape
    tile = ready.shape[1]
    depth = count * width

    def kernel(*refs):
        own_refs, other_refs = refs[:count], refs[count : 2 * count]
        own_w_ref, ready_ref, out_ref, row, other_row = refs[2 * count :]
        for into, group in ((row, own_refs), (other_row, other_refs)):
            for i, ref in enumerate(group):
                into[:, i * width : (i + 1) * width] = ref[...]
        term = jnp.dot(row[...], own_w_ref[:depth, :tile], preferred_element_type=jnp.float32)
        other_term = jnp.dot(
            other_row[...], ready_ref[:depth, :], preferred_element_type=jnp.float32
        )
        out_ref[...] = term + other_term

    vmem = pl.BlockSpec(memory_space=pltpu.VMEM)
    return pl.pallas_call(
        kernel,
        in_specs=[vmem] * (2 * count + 2),
        out_specs=vmem,
        out_shape=pltpu.VMEM((rows, tile), jnp.float32),
        scratch_shapes=[pltpu.VMEM((rows, depth), jnp.bfloat16)] * 2,
        compiler_params=pltpu.CompilerParams(vmem_limit_bytes=8 * MIB),
        cost_estimate=pl.CostEstimate(
            flops=4 * rows * depth * tile, bytes_accessed=4 * MIB, transcendentals=0
        ),
    )(*[in_vmem(x) for x in own + other], in_vmem(own_w), ready)


def project(own, other, own_w, other_w, ready, base, own_base):
    count = len(own)
    rows = own[0].shape[0]
    depth, columns = own_w.shape
    tile = column_tile(columns)
    tiles = columns // tile
    late = tiles - len(ready)

    def kernel(*refs):
        own_refs, other_refs = refs[:count], refs[count : 2 * count]
        own_w_ref, other_w_ref, *refs = refs[2 * count :]
        base_ref, own_base_ref, *refs = refs
        ready_refs, refs = refs[: len(ready)], refs[len(ready) :]
        out_ref, row, other_row, other_base, held, out_sem, w_buf, w_sem = refs

        def place(n):
            return pl.ds(pl.multiple_of(n * tile, tile), tile)

        def give(n):
            return pltpu.make_async_copy(
                held.at[:, place(n)], out_ref.at[:, place(n)], out_sem.at[n]
            )

        def coming(n):
            slot = n - len(ready)
            return tile_copy(other_w_ref, n, w_buf.at[slot], w_sem.at[slot])

        def dot(array, weight, down, place=slice(None)):
            return jnp.dot(
                array[:, down], weight[down, place], preferred_element_type=jnp.float32
            )

        def finish(n, total):
            held[:, place(n)] = total.astype(held.dtype)
            give(n).start()

        def multiply_first(weight):
            down = slice(depth - own_refs[-1].shape[1], depth)
            total = dot(row, own_w_ref, down, place(0)) + dot(other_row, weight, down)
            finish(0, total + base_ref[...])

        def multiply(n, weight):
            half, rest = slice(0, depth // 2), slice(depth // 2, depth)
            other_base[...] = dot(other_row, weight, half)
            term = own_base_ref[:, place(n - 1)] + dot(row, own_w_ref, rest, place(n))
            other_term = other_base[...] + dot(other_row, weight, rest)
            finish(n, term + other_term)

        for n in range(len(ready), tiles):
            coming(n).start()
        for into, group in ((row, own_refs), (other_row, other_refs)):
            for i, ref in enumerate(group):
                width = ref.shape[1]
                into[:, i * width : (i + 1) * width] = ref[...]
        for n, ref in enumerate(ready_refs):
            if n:
                multiply(n, ref)
            else:
                multiply_first(ref)

        @pl.loop(len(ready), tiles)
        def _(n):
            coming(n).wait()
            multiply(n, w_buf.at[n - len(ready)])

        @pl.loop(0, tiles)
        def _(n):
            give(n).wait()

    vmem = pl.BlockSpec(memory_space=pltpu.VMEM)
    hbm = pl.BlockSpec(memory_space=pltpu.HBM)
    return pl.pallas_call(
        kernel,
        in_specs=[vmem] * (2 * count + 1) + [hbm] + [vmem] * (2 + len(ready)),
        out_specs=pl.BlockSpec(memory_space=pl.ANY),
        out_shape=jax.ShapeDtypeStruct((rows, columns), jnp.bfloat16),
        scratch_shapes=[
            pltpu.VMEM((rows, depth), jnp.bfloat16),
            pltpu.VMEM((rows, depth), jnp.bfloat16),
            pltpu.VMEM((rows, tile), jnp.float32),
            pltpu.VMEM((rows, columns), jnp.bfloat16),
            pltpu.SemaphoreType.DMA((tiles,)),
            pltpu.VMEM((late, depth, tile), jnp.bfloat16),
            pltpu.SemaphoreType.DMA((late,)),
        ],
        compiler_params=pltpu.CompilerParams(vmem_limit_bytes=24 * MIB),
        cost_estimate=pl.CostEstimate(
            flops=4 * rows * depth * columns, bytes_accessed=32 * MIB, transcendentals=0
        ),
    )(*[in_vmem(x) for x in own + other], in_vmem(own_w), in_hbm(other_w), base, own_base, *ready)


def shards(queries, keys, values, segments, out_weight):
    rows = queries.shape[0]
    heads_kv = keys.shape[1] // HEAD_SIZE
    peers = lax.axis_size("seq")
    seq_index = lax.axis_index("seq")
    swap = [(0, 1), (1, 0)]

    own = list(pack(keys, values))
    out_weight, own[0] = lax.optimization_barrier((out_weight, own[0]))
    other_w = lax.ppermute(out_weight, "head", swap)
    two_on = [(i, i + 2) for i in range(peers - 2)]
    pair = [(i, i ^ 1) for i in range(peers)]
    odd = seq_index % 2 == 1
    far = [lax.ppermute(x, "seq", two_on) for x in own[:-1]]
    queries, far[0] = lax.optimization_barrier((queries, far[0]))
    marks, queries = prepare(seq_index.astype(jnp.int32).reshape(1), segments, queries)
    far[1], marks = lax.optimization_barrier((far[1], marks))
    upper_w = out_weight
    upper_w, marks = lax.optimization_barrier((upper_w, marks))
    upper_w = stage(upper_w)
    far[2], upper_w = lax.optimization_barrier((far[2], upper_w))
    near = [lax.ppermute(jnp.where(odd, f, x), "seq", pair) for f, x in zip(far, own)]
    beside = lax.ppermute(own[-1], "seq", pair)
    last, far[0] = lax.optimization_barrier((jnp.concatenate([own[-1], beside]), far[0]))
    last = lax.ppermute(last, "seq", two_on)
    far.append(last[:rows])
    near.append(jnp.where(odd, beside, last[rows:]))

    mine, ready = [], []
    for h in range(heads_kv):
        if mine:
            marks, mine[-1] = lax.optimization_barrier((marks, mine[-1]))
        weights = other_w if h == heads_kv - 1 else None
        result, *tile = attend(queries, marks, h, (own[h], near[h], far[h]), weights)
        mine.append(result)
        ready += tile
        if h == heads_kv // 2 - 1:
            own_base = project_own(mine, upper_w, column_tile(out_weight.shape[1]))
            marks, own_base = lax.optimization_barrier((marks, own_base))
    theirs = [lax.ppermute(x, "head", swap) for x in mine]
    base = project_early(mine[:-1], theirs[:-1], out_weight, ready[0])
    return project(mine, theirs, out_weight, other_w, ready, base, own_base)


def solution(mesh):
    placed = (
        P(("groups", "seq"), "head"),
        P(("groups", "seq"), "head"),
        P(("groups", "seq"), "head"),
        P("groups"),
        P("head", None),
    )
    return jax.shard_map(
        shards, mesh=mesh, in_specs=placed, out_specs=P(("groups", "seq"), None), check_vma=False
    )
```

```python
import functools

import jax
import jax.numpy as jnp
from jax import lax
from jax.experimental import pallas as pl
from jax.experimental.pallas import tpu as pltpu
from jax.sharding import PartitionSpec as P

HEAD_SIZE = 128
SCALAR = 168
ATTENTION_SPAN = 1024
TILE = 128
MARK = 128.0
LOG2E = 1.4426950408889634
MIB = 1 << 20
EARLY = 2


def joined(*parts):
    parts = [part for part in parts if part.shape[1]]
    return parts[0] if len(parts) == 1 else jnp.concatenate(parts, axis=1)


def attend_kernel(q_ref, own_ref, near_ref, far_ref, mark_ref, out_ref):
    rows = own_ref.shape[0]
    group = q_ref.shape[1] // HEAD_SIZE
    factor = LOG2E * SCALAR ** (-0.5)
    ones = jnp.ones((rows, HEAD_SIZE), jnp.bfloat16)

    def keys_of(ref, block):
        marks = mark_ref[block * rows : (block + 1) * rows, :]
        return jnp.concatenate([ref[:, :HEAD_SIZE], marks], axis=1)

    def values_of(ref):
        return jnp.concatenate([ref[:, HEAD_SIZE:], ones], axis=1)

    keys = [keys_of(far_ref, 0), keys_of(near_ref, 1), keys_of(own_ref, 2)]
    values = [values_of(far_ref), values_of(near_ref), values_of(own_ref)]
    row = lax.broadcasted_iota(jnp.int32, (TILE, TILE), 0)
    col = lax.broadcasted_iota(jnp.int32, (TILE, TILE), 1)
    inside = jnp.concatenate([col > row] * group, axis=0)
    causal = jnp.concatenate([col <= row] * group, axis=0)

    def score_tile(t):
        span = slice(t * TILE, (t + 1) * TILE)
        marks = mark_ref[2 * rows + t * TILE : 2 * rows + (t + 1) * TILE, :]
        query = jnp.concatenate(
            [
                jnp.concatenate([q_ref[span, g * HEAD_SIZE : (g + 1) * HEAD_SIZE], marks], axis=1)
                for g in range(group)
            ],
            axis=0,
        )
        parts = [keys[0][t * TILE :], keys[1], keys[2][: (t + 1) * TILE]]
        scores = [
            lax.dot_general(
                query, key, (((1,), (1,)), ((), ())), preferred_element_type=jnp.float32
            )
            for key in parts
        ]
        first = jnp.where(inside, scores[0][:, :TILE], -1e30)
        scores[0] = joined(first, *([scores[0][:, TILE:]] if scores[0].shape[1] > TILE else []))
        last = jnp.where(causal, scores[2][:, t * TILE :], -1e30)
        scores[2] = joined(*([scores[2][:, : t * TILE]] if t else []), last)
        return scores

    def weigh_tile(t, scores):
        columns = [
            score[:, c : c + HEAD_SIZE]
            for score in scores
            for c in range(0, score.shape[1], HEAD_SIZE)
        ]
        top = jnp.max(functools.reduce(jnp.maximum, columns), axis=1, keepdims=True)
        return [jnp.exp2((score - top) * factor).astype(jnp.bfloat16) for score in scores]

    def give_tile(t, weights):
        span = slice(t * TILE, (t + 1) * TILE)
        parts = [values[0][t * TILE :], values[1], values[2][: (t + 1) * TILE]]
        total = None
        for weight, value in zip(weights, parts):
            term = jnp.dot(weight, value, preferred_element_type=jnp.float32)
            total = term if total is None else total + term
        result = (total[:, :HEAD_SIZE] / total[:, HEAD_SIZE:]).astype(jnp.bfloat16)
        for g in range(group):
            out_ref[span, g * HEAD_SIZE : (g + 1) * HEAD_SIZE] = result[
                g * TILE : (g + 1) * TILE
            ]

    tiles = rows // TILE
    scores = [score_tile(t) for t in range(tiles)]
    weights = [weigh_tile(t, scores[t]) for t in range(tiles)]
    for t in range(tiles):
        give_tile(t, weights[t])


def in_vmem(x):
    return pltpu.with_memory_space_constraint(x, pltpu.VMEM)


def in_hbm(x):
    return pltpu.with_memory_space_constraint(x, pltpu.HBM)


def pack_kernel(keys_ref, values_ref, *refs):
    outs, sem = refs[:-1], refs[-1]
    copies = []
    for h, out in enumerate(outs):
        for side, ref in enumerate((keys_ref, values_ref)):
            copies.append(
                pltpu.make_async_copy(
                    ref.at[:, h * HEAD_SIZE : (h + 1) * HEAD_SIZE],
                    out.at[:, side * HEAD_SIZE : (side + 1) * HEAD_SIZE],
                    sem.at[h, side],
                )
            )
    for copy in copies:
        copy.start()
    for copy in copies:
        copy.wait()


def pack(keys, values):
    rows, heads = keys.shape[0], keys.shape[1] // HEAD_SIZE
    return pl.pallas_call(
        pack_kernel,
        in_specs=[pl.BlockSpec(memory_space=pltpu.HBM)] * 2,
        out_specs=[pl.BlockSpec(memory_space=pltpu.VMEM)] * heads,
        out_shape=[pltpu.VMEM((rows, 2 * HEAD_SIZE), jnp.bfloat16)] * heads,
        scratch_shapes=[pltpu.SemaphoreType.DMA((heads, 2))],
        compiler_params=pltpu.CompilerParams(vmem_limit_bytes=2 * MIB),
        cost_estimate=pl.CostEstimate(flops=0, bytes_accessed=2 * MIB, transcendentals=0),
    )(in_hbm(keys), in_hbm(values))


def prepare(seq_index, segments, queries):
    rows = queries.shape[0]
    slab = segments.shape[0]
    blocks = 3

    def kernel(index_ref, seg_ref, q_ref, mark_ref, q_out, sem):
        copy = pltpu.make_async_copy(q_ref, q_out, sem)
        copy.start()
        ids = lax.broadcasted_iota(jnp.int32, (HEAD_SIZE, rows), 0)
        for b in range(blocks):
            block = index_ref[0] + b - (blocks - 1)
            seen = seg_ref[pl.ds(jnp.maximum(block, 0), 1), :]
            hit = (seen == ids) & (block >= 0)
            mark = jnp.where(hit, MARK, 0.0)
            mark_ref[b * rows : (b + 1) * rows, :] = mark.T.astype(jnp.bfloat16)
        copy.wait()

    vmem = pl.BlockSpec(memory_space=pltpu.VMEM)
    return pl.pallas_call(
        kernel,
        in_specs=[
            pl.BlockSpec(memory_space=pltpu.SMEM),
            vmem,
            pl.BlockSpec(memory_space=pltpu.HBM),
        ],
        out_specs=[vmem, vmem],
        out_shape=[
            pltpu.VMEM((blocks * rows, HEAD_SIZE), jnp.bfloat16),
            pltpu.VMEM(queries.shape, queries.dtype),
        ],
        scratch_shapes=[pltpu.SemaphoreType.DMA],
        compiler_params=pltpu.CompilerParams(vmem_limit_bytes=4 * MIB),
        cost_estimate=pl.CostEstimate(flops=1024, bytes_accessed=1024, transcendentals=0),
    )(seq_index, segments.reshape(slab // rows, rows), in_hbm(queries))


def column_tile(columns):
    return 768 if columns % 768 == 0 else 128


def tile_copy(weights, n, into, sem):
    tile = into.shape[1]
    place = pl.ds(pl.multiple_of(n * tile, tile), tile)
    return pltpu.make_async_copy(weights.at[:, place], into, sem)


def attend(queries, marks, head, part, weights=None):
    rows = marks.shape[0] // 3
    width = 2 * HEAD_SIZE

    def kernel(q_ref, mark_ref, own_ref, near_ref, far_ref, *refs):
        if weights is None:
            (out_ref,) = refs
        else:
            w_ref, out_ref, *tile_refs, sem = refs
            copies = [tile_copy(w_ref, n, ref, sem.at[n]) for n, ref in enumerate(tile_refs)]
            for copy in copies:
                copy.start()
        left = head * width
        attend_kernel(
            q_ref.at[:, left : left + width], own_ref, near_ref, far_ref, mark_ref, out_ref
        )
        if weights is not None:
            for copy in copies:
                copy.wait()

    vmem = pl.BlockSpec(memory_space=pltpu.VMEM)
    specs, outs = [vmem] * 5, [pltpu.VMEM((rows, width), jnp.bfloat16)]
    flat, scratch = [], []
    if weights is not None:
        depth, columns = weights.shape
        specs.append(pl.BlockSpec(memory_space=pltpu.HBM))
        flat.append(in_hbm(weights))
        outs += [pltpu.VMEM((depth, column_tile(columns)), jnp.bfloat16)] * EARLY
        scratch.append(pltpu.SemaphoreType.DMA((EARLY,)))
    return pl.pallas_call(
        kernel,
        in_specs=specs,
        out_specs=[vmem] * len(outs),
        out_shape=outs,
        scratch_shapes=scratch,
        compiler_params=pltpu.CompilerParams(vmem_limit_bytes=8 * MIB),
        cost_estimate=pl.CostEstimate(flops=1024, bytes_accessed=1024, transcendentals=0),
    )(queries, marks, *[in_vmem(x) for x in part], *flat)


def stage_kernel(in_ref, out_ref, sem, *, skip):
    rows, columns = out_ref.shape
    copy = pltpu.make_async_copy(in_ref.at[:rows, skip : skip + columns], out_ref, sem)
    copy.start()
    copy.wait()


def stage(own_w):
    depth, columns = own_w.shape
    skip = column_tile(columns)
    return pl.pallas_call(
        functools.partial(stage_kernel, skip=skip),
        in_specs=[pl.BlockSpec(memory_space=pltpu.HBM)],
        out_specs=pl.BlockSpec(memory_space=pltpu.VMEM),
        out_shape=pltpu.VMEM((depth // 2, columns - skip), own_w.dtype),
        scratch_shapes=[pltpu.SemaphoreType.DMA],
        compiler_params=pltpu.CompilerParams(vmem_limit_bytes=MIB),
        cost_estimate=pl.CostEstimate(flops=1024, bytes_accessed=1024, transcendentals=0),
    )(in_hbm(own_w))


def project_own(own, upper_w, tile):
    count = len(own)
    rows, width = own[0].shape
    columns = upper_w.shape[1]
    tile *= 2 if columns % (2 * tile) == 0 else 1
    depth = count * width

    def kernel(*refs):
        own_refs, (upper_w_ref, out_ref, row) = refs[:count], refs[count:]
        for i, ref in enumerate(own_refs):
            row[:, i * width : (i + 1) * width] = ref[...]

        @pl.loop(0, columns // tile)
        def _(n):
            place = pl.ds(pl.multiple_of(n * tile, tile), tile)
            out_ref[:, place] = jnp.dot(
                row[...], upper_w_ref[:, place], preferred_element_type=jnp.float32
            )

    vmem = pl.BlockSpec(memory_space=pltpu.VMEM)
    return pl.pallas_call(
        kernel,
        in_specs=[vmem] * (count + 1),
        out_specs=vmem,
        out_shape=pltpu.VMEM((rows, columns), jnp.float32),
        scratch_shapes=[pltpu.VMEM((rows, depth), jnp.bfloat16)],
        compiler_params=pltpu.CompilerParams(vmem_limit_bytes=10 * MIB),
        cost_estimate=pl.CostEstimate(flops=1024, bytes_accessed=1024, transcendentals=0),
    )(*[in_vmem(x) for x in own], upper_w)


def project_early(own, other, own_w, ready):
    count = len(own)
    rows, width = own[0].shape
    tile = ready.shape[1]
    depth = count * width

    def kernel(*refs):
        own_refs, other_refs = refs[:count], refs[count : 2 * count]
        own_w_ref, ready_ref, out_ref, row, other_row = refs[2 * count :]
        for into, group in ((row, own_refs), (other_row, other_refs)):
            for i, ref in enumerate(group):
                into[:, i * width : (i + 1) * width] = ref[...]
        term = jnp.dot(row[...], own_w_ref[:depth, :tile], preferred_element_type=jnp.float32)
        other_term = jnp.dot(
            other_row[...], ready_ref[:depth, :], preferred_element_type=jnp.float32
        )
        out_ref[...] = term + other_term

    vmem = pl.BlockSpec(memory_space=pltpu.VMEM)
    return pl.pallas_call(
        kernel,
        in_specs=[vmem] * (2 * count + 2),
        out_specs=vmem,
        out_shape=pltpu.VMEM((rows, tile), jnp.float32),
        scratch_shapes=[pltpu.VMEM((rows, depth), jnp.bfloat16)] * 2,
        compiler_params=pltpu.CompilerParams(vmem_limit_bytes=8 * MIB),
        cost_estimate=pl.CostEstimate(
            flops=4 * rows * depth * tile, bytes_accessed=4 * MIB, transcendentals=0
        ),
    )(*[in_vmem(x) for x in own + other], in_vmem(own_w), ready)


def project(own, other, own_w, other_w, ready, base, own_base):
    count = len(own)
    rows = own[0].shape[0]
    depth, columns = own_w.shape
    tile = column_tile(columns)
    tiles = columns // tile
    late = tiles - len(ready)

    def kernel(*refs):
        own_refs, other_refs = refs[:count], refs[count : 2 * count]
        own_w_ref, other_w_ref, *refs = refs[2 * count :]
        base_ref, own_base_ref, *refs = refs
        ready_refs, refs = refs[: len(ready)], refs[len(ready) :]
        out_ref, row, other_row, other_base, held, out_sem, w_buf, w_sem = refs

        def place(n):
            return pl.ds(pl.multiple_of(n * tile, tile), tile)

        def give(n):
            return pltpu.make_async_copy(
                held.at[:, place(n)], out_ref.at[:, place(n)], out_sem.at[n]
            )

        def coming(n):
            slot = n - len(ready)
            return tile_copy(other_w_ref, n, w_buf.at[slot], w_sem.at[slot])

        def dot(array, weight, down, place=slice(None)):
            return jnp.dot(
                array[:, down], weight[down, place], preferred_element_type=jnp.float32
            )

        def finish(n, total):
            held[:, place(n)] = total.astype(held.dtype)
            give(n).start()

        def multiply_first(weight):
            down = slice(depth - own_refs[-1].shape[1], depth)
            total = dot(row, own_w_ref, down, place(0)) + dot(other_row, weight, down)
            finish(0, total + base_ref[...])

        def multiply(n, weight):
            half, rest = slice(0, depth // 2), slice(depth // 2, depth)
            other_base[...] = dot(other_row, weight, half)
            term = own_base_ref[:, place(n - 1)] + dot(row, own_w_ref, rest, place(n))
            other_term = other_base[...] + dot(other_row, weight, rest)
            finish(n, term + other_term)

        for n in range(len(ready), tiles):
            coming(n).start()
        for into, group in ((row, own_refs), (other_row, other_refs)):
            for i, ref in enumerate(group):
                width = ref.shape[1]
                into[:, i * width : (i + 1) * width] = ref[...]
        for n, ref in enumerate(ready_refs):
            if n:
                multiply(n, ref)
            else:
                multiply_first(ref)

        @pl.loop(len(ready), tiles)
        def _(n):
            coming(n).wait()
            multiply(n, w_buf.at[n - len(ready)])

        @pl.loop(0, tiles)
        def _(n):
            give(n).wait()

    vmem = pl.BlockSpec(memory_space=pltpu.VMEM)
    hbm = pl.BlockSpec(memory_space=pltpu.HBM)
    return pl.pallas_call(
        kernel,
        in_specs=[vmem] * (2 * count + 1) + [hbm] + [vmem] * (2 + len(ready)),
        out_specs=pl.BlockSpec(memory_space=pl.ANY),
        out_shape=jax.ShapeDtypeStruct((rows, columns), jnp.bfloat16),
        scratch_shapes=[
            pltpu.VMEM((rows, depth), jnp.bfloat16),
            pltpu.VMEM((rows, depth), jnp.bfloat16),
            pltpu.VMEM((rows, tile), jnp.float32),
            pltpu.VMEM((rows, columns), jnp.bfloat16),
            pltpu.SemaphoreType.DMA((tiles,)),
            pltpu.VMEM((late, depth, tile), jnp.bfloat16),
            pltpu.SemaphoreType.DMA((late,)),
        ],
        compiler_params=pltpu.CompilerParams(vmem_limit_bytes=24 * MIB),
        cost_estimate=pl.CostEstimate(
            flops=4 * rows * depth * columns, bytes_accessed=32 * MIB, transcendentals=0
        ),
    )(*[in_vmem(x) for x in own + other], in_vmem(own_w), in_hbm(other_w), base, own_base, *ready)


def shards(queries, keys, values, segments, out_weight):
    rows = queries.shape[0]
    heads_kv = keys.shape[1] // HEAD_SIZE
    peers = lax.axis_size("seq")
    seq_index = lax.axis_index("seq")
    swap = [(0, 1), (1, 0)]

    own = list(pack(keys, values))
    out_weight, own[0] = lax.optimization_barrier((out_weight, own[0]))
    other_w = lax.ppermute(out_weight, "head", swap)
    two_on = [(i, i + 2) for i in range(peers - 2)]
    pair = [(i, i ^ 1) for i in range(peers)]
    odd = seq_index % 2 == 1
    far = [lax.ppermute(x, "seq", two_on) for x in own[:-1]]
    queries, segments, far[0] = lax.optimization_barrier((queries, segments, far[0]))
    marks, queries = prepare(seq_index.astype(jnp.int32).reshape(1), segments, queries)
    upper_w = out_weight
    upper_w, marks = lax.optimization_barrier((upper_w, marks))
    upper_w = stage(upper_w)
    far[2], upper_w = lax.optimization_barrier((far[2], upper_w))
    near = [lax.ppermute(jnp.where(odd, f, x), "seq", pair) for f, x in zip(far, own)]
    beside = lax.ppermute(own[-1], "seq", pair)
    last, far[0] = lax.optimization_barrier((jnp.concatenate([own[-1], beside]), far[0]))
    last = lax.ppermute(last, "seq", two_on)
    far.append(last[:rows])
    near.append(jnp.where(odd, beside, last[rows:]))

    mine, ready = [], []
    for h in range(heads_kv):
        if mine:
            marks, mine[-1] = lax.optimization_barrier((marks, mine[-1]))
        weights = other_w if h == heads_kv - 1 else None
        result, *tile = attend(queries, marks, h, (own[h], near[h], far[h]), weights)
        mine.append(result)
        ready += tile
        if h == heads_kv // 2 - 1:
            own_base = project_own(mine, upper_w, column_tile(out_weight.shape[1]))
            marks, own_base = lax.optimization_barrier((marks, own_base))
    theirs = [lax.ppermute(x, "head", swap) for x in mine]
    base = project_early(mine[:-1], theirs[:-1], out_weight, ready[0])
    return project(mine, theirs, out_weight, other_w, ready, base, own_base)


def solution(mesh):
    placed = (
        P(("groups", "seq"), "head"),
        P(("groups", "seq"), "head"),
        P(("groups", "seq"), "head"),
        P("groups"),
        P("head", None),
    )
    return jax.shard_map(
        shards, mesh=mesh, in_specs=placed, out_specs=P(("groups", "seq"), None), check_vma=False
    )
```

```python
import functools

import jax
import jax.numpy as jnp
from jax import lax
from jax.experimental import pallas as pl
from jax.experimental.pallas import tpu as pltpu
from jax.sharding import PartitionSpec as P

HEAD_SIZE = 128
SCALAR = 168
ATTENTION_SPAN = 1024
TILE = 128
MARK = 128.0
LOG2E = 1.4426950408889634
MIB = 1 << 20
EARLY = 2


def joined(*parts):
    parts = [part for part in parts if part.shape[1]]
    return parts[0] if len(parts) == 1 else jnp.concatenate(parts, axis=1)


def attend_kernel(q_ref, own_ref, near_ref, far_ref, mark_ref, out_ref):
    rows = own_ref.shape[0]
    group = q_ref.shape[1] // HEAD_SIZE
    factor = LOG2E * SCALAR ** (-0.5)
    ones = jnp.ones((rows, HEAD_SIZE), jnp.bfloat16)

    def keys_of(ref, block):
        marks = mark_ref[block * rows : (block + 1) * rows, :]
        return jnp.concatenate([ref[:, :HEAD_SIZE], marks], axis=1)

    def values_of(ref):
        return jnp.concatenate([ref[:, HEAD_SIZE:], ones], axis=1)

    keys = [keys_of(far_ref, 0), keys_of(near_ref, 1), keys_of(own_ref, 2)]
    values = [values_of(far_ref), values_of(near_ref), values_of(own_ref)]
    row = lax.broadcasted_iota(jnp.int32, (TILE, TILE), 0)
    col = lax.broadcasted_iota(jnp.int32, (TILE, TILE), 1)
    inside = jnp.concatenate([col > row] * group, axis=0)
    causal = jnp.concatenate([col <= row] * group, axis=0)

    def score_tile(t):
        span = slice(t * TILE, (t + 1) * TILE)
        marks = mark_ref[2 * rows + t * TILE : 2 * rows + (t + 1) * TILE, :]
        query = jnp.concatenate(
            [
                jnp.concatenate([q_ref[span, g * HEAD_SIZE : (g + 1) * HEAD_SIZE], marks], axis=1)
                for g in range(group)
            ],
            axis=0,
        )
        parts = [keys[0][t * TILE :], keys[1], keys[2][: (t + 1) * TILE]]
        scores = [
            lax.dot_general(
                query, key, (((1,), (1,)), ((), ())), preferred_element_type=jnp.float32
            )
            for key in parts
        ]
        first = jnp.where(inside, scores[0][:, :TILE], -1e30)
        scores[0] = joined(first, *([scores[0][:, TILE:]] if scores[0].shape[1] > TILE else []))
        last = jnp.where(causal, scores[2][:, t * TILE :], -1e30)
        scores[2] = joined(*([scores[2][:, : t * TILE]] if t else []), last)
        return scores

    def weigh_tile(t, scores):
        columns = [
            score[:, c : c + HEAD_SIZE]
            for score in scores
            for c in range(0, score.shape[1], HEAD_SIZE)
        ]
        top = jnp.max(functools.reduce(jnp.maximum, columns), axis=1, keepdims=True)
        return [jnp.exp2((score - top) * factor).astype(jnp.bfloat16) for score in scores]

    def give_tile(t, weights):
        span = slice(t * TILE, (t + 1) * TILE)
        parts = [values[0][t * TILE :], values[1], values[2][: (t + 1) * TILE]]
        total = None
        for weight, value in zip(weights, parts):
            term = jnp.dot(weight, value, preferred_element_type=jnp.float32)
            total = term if total is None else total + term
        result = (total[:, :HEAD_SIZE] / total[:, HEAD_SIZE:]).astype(jnp.bfloat16)
        for g in range(group):
            out_ref[span, g * HEAD_SIZE : (g + 1) * HEAD_SIZE] = result[
                g * TILE : (g + 1) * TILE
            ]

    tiles = rows // TILE
    scores = [score_tile(t) for t in range(tiles)]
    weights = [weigh_tile(t, scores[t]) for t in range(tiles)]
    for t in range(tiles):
        give_tile(t, weights[t])


def in_vmem(x):
    return pltpu.with_memory_space_constraint(x, pltpu.VMEM)


def in_hbm(x):
    return pltpu.with_memory_space_constraint(x, pltpu.HBM)


def pack_kernel(keys_ref, values_ref, *refs):
    outs, sem = refs[:-1], refs[-1]
    copies = []
    for h, out in enumerate(outs):
        for side, ref in enumerate((keys_ref, values_ref)):
            copies.append(
                pltpu.make_async_copy(
                    ref.at[:, h * HEAD_SIZE : (h + 1) * HEAD_SIZE],
                    out.at[:, side * HEAD_SIZE : (side + 1) * HEAD_SIZE],
                    sem.at[h, side],
                )
            )
    for copy in copies:
        copy.start()
    for copy in copies:
        copy.wait()


def pack(keys, values):
    rows, heads = keys.shape[0], keys.shape[1] // HEAD_SIZE
    return pl.pallas_call(
        pack_kernel,
        in_specs=[pl.BlockSpec(memory_space=pltpu.HBM)] * 2,
        out_specs=[pl.BlockSpec(memory_space=pltpu.VMEM)] * heads,
        out_shape=[pltpu.VMEM((rows, 2 * HEAD_SIZE), jnp.bfloat16)] * heads,
        scratch_shapes=[pltpu.SemaphoreType.DMA((heads, 2))],
        compiler_params=pltpu.CompilerParams(vmem_limit_bytes=2 * MIB),
        cost_estimate=pl.CostEstimate(flops=0, bytes_accessed=2 * MIB, transcendentals=0),
    )(in_hbm(keys), in_hbm(values))


def prepare(seq_index, segments, queries):
    rows = queries.shape[0]
    slab = segments.shape[0]
    blocks = 3

    def kernel(index_ref, seg_ref, q_ref, mark_ref, q_out, sem):
        copy = pltpu.make_async_copy(q_ref, q_out, sem)
        copy.start()
        ids = lax.broadcasted_iota(jnp.int32, (HEAD_SIZE, HEAD_SIZE), 0)
        pieces = rows // HEAD_SIZE
        for b in range(blocks):
            block = index_ref[0] + b - (blocks - 1)
            for p in range(pieces):
                seen = seg_ref[pl.ds(jnp.maximum(block, 0) * pieces + p, 1), :]
                hit = (seen == ids) & (block >= 0)
                mark = jnp.where(hit, MARK, 0.0)
                at = b * rows + p * HEAD_SIZE
                mark_ref[at : at + HEAD_SIZE, :] = mark.T.astype(jnp.bfloat16)
        copy.wait()

    vmem = pl.BlockSpec(memory_space=pltpu.VMEM)
    return pl.pallas_call(
        kernel,
        in_specs=[
            pl.BlockSpec(memory_space=pltpu.SMEM),
            vmem,
            pl.BlockSpec(memory_space=pltpu.HBM),
        ],
        out_specs=[vmem, vmem],
        out_shape=[
            pltpu.VMEM((blocks * rows, HEAD_SIZE), jnp.bfloat16),
            pltpu.VMEM(queries.shape, queries.dtype),
        ],
        scratch_shapes=[pltpu.SemaphoreType.DMA],
        compiler_params=pltpu.CompilerParams(vmem_limit_bytes=4 * MIB),
        cost_estimate=pl.CostEstimate(flops=1024, bytes_accessed=1024, transcendentals=0),
    )(seq_index, segments.reshape(slab // HEAD_SIZE, HEAD_SIZE), in_hbm(queries))


def column_tile(columns):
    return 768 if columns % 768 == 0 else 128


def tile_copy(weights, n, into, sem):
    tile = into.shape[1]
    place = pl.ds(pl.multiple_of(n * tile, tile), tile)
    return pltpu.make_async_copy(weights.at[:, place], into, sem)


def attend(queries, marks, head, part, weights=None):
    rows = marks.shape[0] // 3
    width = 2 * HEAD_SIZE

    def kernel(q_ref, mark_ref, own_ref, near_ref, far_ref, *refs):
        if weights is None:
            (out_ref,) = refs
        else:
            w_ref, out_ref, *tile_refs, sem = refs
            copies = [tile_copy(w_ref, n, ref, sem.at[n]) for n, ref in enumerate(tile_refs)]
            for copy in copies:
                copy.start()
        left = head * width
        attend_kernel(
            q_ref.at[:, left : left + width], own_ref, near_ref, far_ref, mark_ref, out_ref
        )
        if weights is not None:
            for copy in copies:
                copy.wait()

    vmem = pl.BlockSpec(memory_space=pltpu.VMEM)
    specs, outs = [vmem] * 5, [pltpu.VMEM((rows, width), jnp.bfloat16)]
    flat, scratch = [], []
    if weights is not None:
        depth, columns = weights.shape
        specs.append(pl.BlockSpec(memory_space=pltpu.HBM))
        flat.append(in_hbm(weights))
        outs += [pltpu.VMEM((depth, column_tile(columns)), jnp.bfloat16)] * EARLY
        scratch.append(pltpu.SemaphoreType.DMA((EARLY,)))
    return pl.pallas_call(
        kernel,
        in_specs=specs,
        out_specs=[vmem] * len(outs),
        out_shape=outs,
        scratch_shapes=scratch,
        compiler_params=pltpu.CompilerParams(vmem_limit_bytes=8 * MIB),
        cost_estimate=pl.CostEstimate(flops=1024, bytes_accessed=1024, transcendentals=0),
    )(queries, marks, *[in_vmem(x) for x in part], *flat)


def stage_kernel(in_ref, out_ref, sem, *, skip):
    rows, columns = out_ref.shape
    copy = pltpu.make_async_copy(in_ref.at[:rows, skip : skip + columns], out_ref, sem)
    copy.start()
    copy.wait()


def stage(own_w):
    depth, columns = own_w.shape
    skip = column_tile(columns)
    return pl.pallas_call(
        functools.partial(stage_kernel, skip=skip),
        in_specs=[pl.BlockSpec(memory_space=pltpu.HBM)],
        out_specs=pl.BlockSpec(memory_space=pltpu.VMEM),
        out_shape=pltpu.VMEM((depth // 2, columns - skip), own_w.dtype),
        scratch_shapes=[pltpu.SemaphoreType.DMA],
        compiler_params=pltpu.CompilerParams(vmem_limit_bytes=MIB),
        cost_estimate=pl.CostEstimate(flops=1024, bytes_accessed=1024, transcendentals=0),
    )(in_hbm(own_w))


def project_own(own, upper_w, tile):
    count = len(own)
    rows, width = own[0].shape
    columns = upper_w.shape[1]
    tile *= 2 if columns % (2 * tile) == 0 else 1
    depth = count * width

    def kernel(*refs):
        own_refs, (upper_w_ref, out_ref, row) = refs[:count], refs[count:]
        for i, ref in enumerate(own_refs):
            row[:, i * width : (i + 1) * width] = ref[...]

        @pl.loop(0, columns // tile)
        def _(n):
            place = pl.ds(pl.multiple_of(n * tile, tile), tile)
            out_ref[:, place] = jnp.dot(
                row[...], upper_w_ref[:, place], preferred_element_type=jnp.float32
            )

    vmem = pl.BlockSpec(memory_space=pltpu.VMEM)
    return pl.pallas_call(
        kernel,
        in_specs=[vmem] * (count + 1),
        out_specs=vmem,
        out_shape=pltpu.VMEM((rows, columns), jnp.float32),
        scratch_shapes=[pltpu.VMEM((rows, depth), jnp.bfloat16)],
        compiler_params=pltpu.CompilerParams(vmem_limit_bytes=10 * MIB),
        cost_estimate=pl.CostEstimate(flops=1024, bytes_accessed=1024, transcendentals=0),
    )(*[in_vmem(x) for x in own], upper_w)


def project_early(own, other, own_w, ready):
    count = len(own)
    rows, width = own[0].shape
    tile = ready.shape[1]
    depth = count * width

    def kernel(*refs):
        own_refs, other_refs = refs[:count], refs[count : 2 * count]
        own_w_ref, ready_ref, out_ref, row, other_row = refs[2 * count :]
        for into, group in ((row, own_refs), (other_row, other_refs)):
            for i, ref in enumerate(group):
                into[:, i * width : (i + 1) * width] = ref[...]
        term = jnp.dot(row[...], own_w_ref[:depth, :tile], preferred_element_type=jnp.float32)
        other_term = jnp.dot(
            other_row[...], ready_ref[:depth, :], preferred_element_type=jnp.float32
        )
        out_ref[...] = term + other_term

    vmem = pl.BlockSpec(memory_space=pltpu.VMEM)
    return pl.pallas_call(
        kernel,
        in_specs=[vmem] * (2 * count + 2),
        out_specs=vmem,
        out_shape=pltpu.VMEM((rows, tile), jnp.float32),
        scratch_shapes=[pltpu.VMEM((rows, depth), jnp.bfloat16)] * 2,
        compiler_params=pltpu.CompilerParams(vmem_limit_bytes=8 * MIB),
        cost_estimate=pl.CostEstimate(
            flops=4 * rows * depth * tile, bytes_accessed=4 * MIB, transcendentals=0
        ),
    )(*[in_vmem(x) for x in own + other], in_vmem(own_w), ready)


def project(own, other, own_w, other_w, ready, base, own_base):
    count = len(own)
    rows = own[0].shape[0]
    depth, columns = own_w.shape
    tile = column_tile(columns)
    tiles = columns // tile
    late = tiles - len(ready)

    def kernel(*refs):
        own_refs, other_refs = refs[:count], refs[count : 2 * count]
        own_w_ref, other_w_ref, *refs = refs[2 * count :]
        base_ref, own_base_ref, *refs = refs
        ready_refs, refs = refs[: len(ready)], refs[len(ready) :]
        out_ref, row, other_row, other_base, held, out_sem, w_buf, w_sem = refs

        def place(n):
            return pl.ds(pl.multiple_of(n * tile, tile), tile)

        def give(n):
            return pltpu.make_async_copy(
                held.at[:, place(n)], out_ref.at[:, place(n)], out_sem.at[n]
            )

        def coming(n):
            slot = n - len(ready)
            return tile_copy(other_w_ref, n, w_buf.at[slot], w_sem.at[slot])

        def dot(array, weight, down, place=slice(None)):
            return jnp.dot(
                array[:, down], weight[down, place], preferred_element_type=jnp.float32
            )

        def finish(n, total):
            held[:, place(n)] = total.astype(held.dtype)
            give(n).start()

        def multiply_first(weight):
            down = slice(depth - own_refs[-1].shape[1], depth)
            total = dot(row, own_w_ref, down, place(0)) + dot(other_row, weight, down)
            finish(0, total + base_ref[...])

        def multiply(n, weight):
            half, rest = slice(0, depth // 2), slice(depth // 2, depth)
            other_base[...] = dot(other_row, weight, half)
            term = own_base_ref[:, place(n - 1)] + dot(row, own_w_ref, rest, place(n))
            other_term = other_base[...] + dot(other_row, weight, rest)
            finish(n, term + other_term)

        for n in range(len(ready), tiles):
            coming(n).start()
        for into, group in ((row, own_refs), (other_row, other_refs)):
            for i, ref in enumerate(group):
                width = ref.shape[1]
                into[:, i * width : (i + 1) * width] = ref[...]
        for n, ref in enumerate(ready_refs):
            if n:
                multiply(n, ref)
            else:
                multiply_first(ref)

        @pl.loop(len(ready), tiles)
        def _(n):
            coming(n).wait()
            multiply(n, w_buf.at[n - len(ready)])

        @pl.loop(0, tiles)
        def _(n):
            give(n).wait()

    vmem = pl.BlockSpec(memory_space=pltpu.VMEM)
    hbm = pl.BlockSpec(memory_space=pltpu.HBM)
    return pl.pallas_call(
        kernel,
        in_specs=[vmem] * (2 * count + 1) + [hbm] + [vmem] * (2 + len(ready)),
        out_specs=pl.BlockSpec(memory_space=pl.ANY),
        out_shape=jax.ShapeDtypeStruct((rows, columns), jnp.bfloat16),
        scratch_shapes=[
            pltpu.VMEM((rows, depth), jnp.bfloat16),
            pltpu.VMEM((rows, depth), jnp.bfloat16),
            pltpu.VMEM((rows, tile), jnp.float32),
            pltpu.VMEM((rows, columns), jnp.bfloat16),
            pltpu.SemaphoreType.DMA((tiles,)),
            pltpu.VMEM((late, depth, tile), jnp.bfloat16),
            pltpu.SemaphoreType.DMA((late,)),
        ],
        compiler_params=pltpu.CompilerParams(vmem_limit_bytes=24 * MIB),
        cost_estimate=pl.CostEstimate(
            flops=4 * rows * depth * columns, bytes_accessed=32 * MIB, transcendentals=0
        ),
    )(*[in_vmem(x) for x in own + other], in_vmem(own_w), in_hbm(other_w), base, own_base, *ready)


def shards(queries, keys, values, segments, out_weight):
    rows = queries.shape[0]
    heads_kv = keys.shape[1] // HEAD_SIZE
    peers = lax.axis_size("seq")
    seq_index = lax.axis_index("seq")
    swap = [(0, 1), (1, 0)]

    own = list(pack(keys, values))
    out_weight, own[0] = lax.optimization_barrier((out_weight, own[0]))
    other_w = lax.ppermute(out_weight, "head", swap)
    two_on = [(i, i + 2) for i in range(peers - 2)]
    pair = [(i, i ^ 1) for i in range(peers)]
    odd = seq_index % 2 == 1
    far = [lax.ppermute(x, "seq", two_on) for x in own[:-1]]
    queries, segments, far[0] = lax.optimization_barrier((queries, segments, far[0]))
    marks, queries = prepare(seq_index.astype(jnp.int32).reshape(1), segments, queries)
    upper_w = out_weight
    upper_w, marks = lax.optimization_barrier((upper_w, marks))
    upper_w = stage(upper_w)
    far[2], upper_w = lax.optimization_barrier((far[2], upper_w))
    near = [lax.ppermute(jnp.where(odd, f, x), "seq", pair) for f, x in zip(far, own)]
    beside = lax.ppermute(own[-1], "seq", pair)
    last, far[0] = lax.optimization_barrier((jnp.concatenate([own[-1], beside]), far[0]))
    last = lax.ppermute(last, "seq", two_on)
    far.append(last[:rows])
    near.append(jnp.where(odd, beside, last[rows:]))

    mine, ready = [], []
    for h in range(heads_kv):
        if mine:
            marks, mine[-1] = lax.optimization_barrier((marks, mine[-1]))
        weights = other_w if h == heads_kv - 1 else None
        result, *tile = attend(queries, marks, h, (own[h], near[h], far[h]), weights)
        mine.append(result)
        ready += tile
        if h == heads_kv // 2 - 1:
            own_base = project_own(mine, upper_w, column_tile(out_weight.shape[1]))
            marks, own_base = lax.optimization_barrier((marks, own_base))
    theirs = [lax.ppermute(x, "head", swap) for x in mine]
    base = project_early(mine[:-1], theirs[:-1], out_weight, ready[0])
    return project(mine, theirs, out_weight, other_w, ready, base, own_base)


def solution(mesh):
    placed = (
        P(("groups", "seq"), "head"),
        P(("groups", "seq"), "head"),
        P(("groups", "seq"), "head"),
        P("groups"),
        P("head", None),
    )
    return jax.shard_map(
        shards, mesh=mesh, in_specs=placed, out_specs=P(("groups", "seq"), None), check_vma=False
    )
```

```python
import functools

import jax
import jax.numpy as jnp
from jax import lax
from jax.experimental import pallas as pl
from jax.experimental.pallas import tpu as pltpu
from jax.sharding import PartitionSpec as P

HEAD_SIZE = 128
SCALAR = 168
ATTENTION_SPAN = 1024
TILE = 128
MARK = 128.0
LOG2E = 1.4426950408889634
MIB = 1 << 20
EARLY = 2


def joined(*parts):
    parts = [part for part in parts if part.shape[1]]
    return parts[0] if len(parts) == 1 else jnp.concatenate(parts, axis=1)


def attend_kernel(q_ref, own_ref, near_ref, far_ref, mark_ref, out_ref):
    rows = own_ref.shape[0]
    group = q_ref.shape[1] // HEAD_SIZE
    factor = LOG2E * SCALAR ** (-0.5)
    ones = jnp.ones((rows, HEAD_SIZE), jnp.bfloat16)

    def keys_of(ref, block):
        marks = mark_ref[block * rows : (block + 1) * rows, :]
        return jnp.concatenate([ref[:, :HEAD_SIZE], marks], axis=1)

    def values_of(ref):
        return jnp.concatenate([ref[:, HEAD_SIZE:], ones], axis=1)

    keys = [keys_of(far_ref, 0), keys_of(near_ref, 1), keys_of(own_ref, 2)]
    values = [values_of(far_ref), values_of(near_ref), values_of(own_ref)]
    row = lax.broadcasted_iota(jnp.int32, (TILE, TILE), 0)
    col = lax.broadcasted_iota(jnp.int32, (TILE, TILE), 1)
    inside = jnp.concatenate([col > row] * group, axis=0)
    causal = jnp.concatenate([col <= row] * group, axis=0)

    def score_tile(t):
        span = slice(t * TILE, (t + 1) * TILE)
        marks = mark_ref[2 * rows + t * TILE : 2 * rows + (t + 1) * TILE, :]
        query = jnp.concatenate(
            [
                jnp.concatenate([q_ref[span, g * HEAD_SIZE : (g + 1) * HEAD_SIZE], marks], axis=1)
                for g in range(group)
            ],
            axis=0,
        )
        parts = [keys[0][t * TILE :], keys[1], keys[2][: (t + 1) * TILE]]
        scores = [
            lax.dot_general(
                query, key, (((1,), (1,)), ((), ())), preferred_element_type=jnp.float32
            )
            for key in parts
        ]
        first = jnp.where(inside, scores[0][:, :TILE], -1e30)
        scores[0] = joined(first, *([scores[0][:, TILE:]] if scores[0].shape[1] > TILE else []))
        last = jnp.where(causal, scores[2][:, t * TILE :], -1e30)
        scores[2] = joined(*([scores[2][:, : t * TILE]] if t else []), last)
        return scores

    def weigh_tile(t, scores):
        columns = [
            score[:, c : c + HEAD_SIZE]
            for score in scores
            for c in range(0, score.shape[1], HEAD_SIZE)
        ]
        top = jnp.max(functools.reduce(jnp.maximum, columns), axis=1, keepdims=True)
        return [jnp.exp2((score - top) * factor).astype(jnp.bfloat16) for score in scores]

    def give_tile(t, weights):
        span = slice(t * TILE, (t + 1) * TILE)
        parts = [values[0][t * TILE :], values[1], values[2][: (t + 1) * TILE]]
        total = None
        for weight, value in zip(weights, parts):
            term = jnp.dot(weight, value, preferred_element_type=jnp.float32)
            total = term if total is None else total + term
        result = (total[:, :HEAD_SIZE] / total[:, HEAD_SIZE:]).astype(jnp.bfloat16)
        for g in range(group):
            out_ref[span, g * HEAD_SIZE : (g + 1) * HEAD_SIZE] = result[
                g * TILE : (g + 1) * TILE
            ]

    tiles = rows // TILE
    scores = [score_tile(t) for t in range(tiles)]
    weights = [weigh_tile(t, scores[t]) for t in range(tiles)]
    for t in range(tiles):
        give_tile(t, weights[t])


def in_vmem(x):
    return pltpu.with_memory_space_constraint(x, pltpu.VMEM)


def in_hbm(x):
    return pltpu.with_memory_space_constraint(x, pltpu.HBM)


def pack_kernel(keys_ref, values_ref, *refs):
    outs, sem = refs[:-1], refs[-1]
    copies = []
    for h, out in enumerate(outs):
        for side, ref in enumerate((keys_ref, values_ref)):
            copies.append(
                pltpu.make_async_copy(
                    ref.at[:, h * HEAD_SIZE : (h + 1) * HEAD_SIZE],
                    out.at[:, side * HEAD_SIZE : (side + 1) * HEAD_SIZE],
                    sem.at[h, side],
                )
            )
    for copy in copies:
        copy.start()
    for copy in copies:
        copy.wait()


def pack(keys, values):
    rows, heads = keys.shape[0], keys.shape[1] // HEAD_SIZE
    return pl.pallas_call(
        pack_kernel,
        in_specs=[pl.BlockSpec(memory_space=pltpu.HBM)] * 2,
        out_specs=[pl.BlockSpec(memory_space=pltpu.VMEM)] * heads,
        out_shape=[pltpu.VMEM((rows, 2 * HEAD_SIZE), jnp.bfloat16)] * heads,
        scratch_shapes=[pltpu.SemaphoreType.DMA((heads, 2))],
        compiler_params=pltpu.CompilerParams(vmem_limit_bytes=2 * MIB),
        cost_estimate=pl.CostEstimate(flops=0, bytes_accessed=2 * MIB, transcendentals=0),
    )(in_hbm(keys), in_hbm(values))


def prepare(seq_index, segments, queries):
    rows = queries.shape[0]
    slab = segments.shape[0]
    blocks = 3

    def kernel(index_ref, seg_ref, q_ref, mark_ref, q_out, sem):
        copy = pltpu.make_async_copy(q_ref, q_out, sem)
        copy.start()
        ids = lax.broadcasted_iota(jnp.int32, (HEAD_SIZE, HEAD_SIZE), 0)
        pieces = rows // HEAD_SIZE
        for b in range(blocks):
            block = index_ref[0] + b - (blocks - 1)
            for p in range(pieces):
                seen = seg_ref[pl.ds(jnp.maximum(block, 0) * pieces + p, 1), :]
                hit = (seen == ids) & (block >= 0)
                mark = jnp.where(hit, MARK, 0.0)
                at = b * rows + p * HEAD_SIZE
                mark_ref[at : at + HEAD_SIZE, :] = mark.T.astype(jnp.bfloat16)
        copy.wait()

    vmem = pl.BlockSpec(memory_space=pltpu.VMEM)
    return pl.pallas_call(
        kernel,
        in_specs=[
            pl.BlockSpec(memory_space=pltpu.SMEM),
            vmem,
            pl.BlockSpec(memory_space=pltpu.HBM),
        ],
        out_specs=[vmem, vmem],
        out_shape=[
            pltpu.VMEM((blocks * rows, HEAD_SIZE), jnp.bfloat16),
            pltpu.VMEM(queries.shape, queries.dtype),
        ],
        scratch_shapes=[pltpu.SemaphoreType.DMA],
        compiler_params=pltpu.CompilerParams(vmem_limit_bytes=4 * MIB),
        cost_estimate=pl.CostEstimate(flops=1024, bytes_accessed=1024, transcendentals=0),
    )(seq_index, segments.reshape(slab // HEAD_SIZE, HEAD_SIZE), in_hbm(queries))


def column_tile(columns):
    return 768 if columns % 768 == 0 else 128


def tile_copy(weights, n, into, sem):
    tile = into.shape[1]
    place = pl.ds(pl.multiple_of(n * tile, tile), tile)
    return pltpu.make_async_copy(weights.at[:, place], into, sem)


def attend(queries, marks, head, part, weights=None):
    rows = marks.shape[0] // 3
    width = 2 * HEAD_SIZE

    def kernel(q_ref, mark_ref, own_ref, near_ref, far_ref, *refs):
        if weights is None:
            (out_ref,) = refs
        else:
            w_ref, out_ref, *tile_refs, sem = refs
            copies = [tile_copy(w_ref, n, ref, sem.at[n]) for n, ref in enumerate(tile_refs)]
            for copy in copies:
                copy.start()
        left = head * width
        attend_kernel(
            q_ref.at[:, left : left + width], own_ref, near_ref, far_ref, mark_ref, out_ref
        )
        if weights is not None:
            for copy in copies:
                copy.wait()

    vmem = pl.BlockSpec(memory_space=pltpu.VMEM)
    specs, outs = [vmem] * 5, [pltpu.VMEM((rows, width), jnp.bfloat16)]
    flat, scratch = [], []
    if weights is not None:
        depth, columns = weights.shape
        specs.append(pl.BlockSpec(memory_space=pltpu.HBM))
        flat.append(in_hbm(weights))
        outs += [pltpu.VMEM((depth, column_tile(columns)), jnp.bfloat16)] * EARLY
        scratch.append(pltpu.SemaphoreType.DMA((EARLY,)))
    return pl.pallas_call(
        kernel,
        in_specs=specs,
        out_specs=[vmem] * len(outs),
        out_shape=outs,
        scratch_shapes=scratch,
        compiler_params=pltpu.CompilerParams(vmem_limit_bytes=8 * MIB),
        cost_estimate=pl.CostEstimate(flops=1024, bytes_accessed=1024, transcendentals=0),
    )(queries, marks, *[in_vmem(x) for x in part], *flat)


def stage_kernel(in_ref, out_ref, sem, *, skip):
    rows, columns = out_ref.shape
    copy = pltpu.make_async_copy(in_ref.at[:rows, skip : skip + columns], out_ref, sem)
    copy.start()
    copy.wait()


def stage(own_w):
    depth, columns = own_w.shape
    skip = column_tile(columns)
    return pl.pallas_call(
        functools.partial(stage_kernel, skip=skip),
        in_specs=[pl.BlockSpec(memory_space=pltpu.HBM)],
        out_specs=pl.BlockSpec(memory_space=pltpu.VMEM),
        out_shape=pltpu.VMEM((depth // 2, columns - skip), own_w.dtype),
        scratch_shapes=[pltpu.SemaphoreType.DMA],
        compiler_params=pltpu.CompilerParams(vmem_limit_bytes=MIB),
        cost_estimate=pl.CostEstimate(flops=1024, bytes_accessed=1024, transcendentals=0),
    )(in_hbm(own_w))


def project_own(own, upper_w, tile):
    count = len(own)
    rows, width = own[0].shape
    columns = upper_w.shape[1]
    tile *= 2 if columns % (2 * tile) == 0 else 1
    depth = count * width

    def kernel(*refs):
        own_refs, (upper_w_ref, out_ref, row) = refs[:count], refs[count:]
        for i, ref in enumerate(own_refs):
            row[:, i * width : (i + 1) * width] = ref[...]

        for n in range(columns // tile):
            place = slice(n * tile, (n + 1) * tile)
            out_ref[:, place] = jnp.dot(
                row[...], upper_w_ref[:, place], preferred_element_type=jnp.float32
            )

    vmem = pl.BlockSpec(memory_space=pltpu.VMEM)
    return pl.pallas_call(
        kernel,
        in_specs=[vmem] * (count + 1),
        out_specs=vmem,
        out_shape=pltpu.VMEM((rows, columns), jnp.float32),
        scratch_shapes=[pltpu.VMEM((rows, depth), jnp.bfloat16)],
        compiler_params=pltpu.CompilerParams(vmem_limit_bytes=10 * MIB),
        cost_estimate=pl.CostEstimate(flops=1024, bytes_accessed=1024, transcendentals=0),
    )(*[in_vmem(x) for x in own], upper_w)


def project_early(own, other, own_w, ready):
    count = len(own)
    rows, width = own[0].shape
    tile = ready.shape[1]
    depth = count * width

    def kernel(*refs):
        own_refs, other_refs = refs[:count], refs[count : 2 * count]
        own_w_ref, ready_ref, out_ref, row, other_row = refs[2 * count :]
        for into, group in ((row, own_refs), (other_row, other_refs)):
            for i, ref in enumerate(group):
                into[:, i * width : (i + 1) * width] = ref[...]
        term = jnp.dot(row[...], own_w_ref[:depth, :tile], preferred_element_type=jnp.float32)
        other_term = jnp.dot(
            other_row[...], ready_ref[:depth, :], preferred_element_type=jnp.float32
        )
        out_ref[...] = term + other_term

    vmem = pl.BlockSpec(memory_space=pltpu.VMEM)
    return pl.pallas_call(
        kernel,
        in_specs=[vmem] * (2 * count + 2),
        out_specs=vmem,
        out_shape=pltpu.VMEM((rows, tile), jnp.float32),
        scratch_shapes=[pltpu.VMEM((rows, depth), jnp.bfloat16)] * 2,
        compiler_params=pltpu.CompilerParams(vmem_limit_bytes=8 * MIB),
        cost_estimate=pl.CostEstimate(
            flops=4 * rows * depth * tile, bytes_accessed=4 * MIB, transcendentals=0
        ),
    )(*[in_vmem(x) for x in own + other], in_vmem(own_w), ready)


def project(own, other, own_w, other_w, ready, base, own_base):
    count = len(own)
    rows = own[0].shape[0]
    depth, columns = own_w.shape
    tile = column_tile(columns)
    tiles = columns // tile
    late = tiles - len(ready)

    def kernel(*refs):
        own_refs, other_refs = refs[:count], refs[count : 2 * count]
        own_w_ref, other_w_ref, *refs = refs[2 * count :]
        base_ref, own_base_ref, *refs = refs
        ready_refs, refs = refs[: len(ready)], refs[len(ready) :]
        out_ref, row, other_row, other_base, held, out_sem, w_buf, w_sem = refs

        def place(n):
            return pl.ds(pl.multiple_of(n * tile, tile), tile)

        def give(n):
            return pltpu.make_async_copy(
                held.at[:, place(n)], out_ref.at[:, place(n)], out_sem.at[n]
            )

        def coming(n):
            slot = n - len(ready)
            return tile_copy(other_w_ref, n, w_buf.at[slot], w_sem.at[slot])

        def dot(array, weight, down, place=slice(None)):
            return jnp.dot(
                array[:, down], weight[down, place], preferred_element_type=jnp.float32
            )

        def finish(n, total):
            held[:, place(n)] = total.astype(held.dtype)
            give(n).start()

        def multiply_first(weight):
            down = slice(depth - own_refs[-1].shape[1], depth)
            total = dot(row, own_w_ref, down, place(0)) + dot(other_row, weight, down)
            finish(0, total + base_ref[...])

        def multiply(n, weight):
            half, rest = slice(0, depth // 2), slice(depth // 2, depth)
            other_base[...] = dot(other_row, weight, half)
            term = own_base_ref[:, place(n - 1)] + dot(row, own_w_ref, rest, place(n))
            other_term = other_base[...] + dot(other_row, weight, rest)
            finish(n, term + other_term)

        for n in range(len(ready), tiles):
            coming(n).start()
        for into, group in ((row, own_refs), (other_row, other_refs)):
            for i, ref in enumerate(group):
                width = ref.shape[1]
                into[:, i * width : (i + 1) * width] = ref[...]
        for n, ref in enumerate(ready_refs):
            if n:
                multiply(n, ref)
            else:
                multiply_first(ref)

        @pl.loop(len(ready), tiles)
        def _(n):
            coming(n).wait()
            multiply(n, w_buf.at[n - len(ready)])

        @pl.loop(0, tiles)
        def _(n):
            give(n).wait()

    vmem = pl.BlockSpec(memory_space=pltpu.VMEM)
    hbm = pl.BlockSpec(memory_space=pltpu.HBM)
    return pl.pallas_call(
        kernel,
        in_specs=[vmem] * (2 * count + 1) + [hbm] + [vmem] * (2 + len(ready)),
        out_specs=pl.BlockSpec(memory_space=pl.ANY),
        out_shape=jax.ShapeDtypeStruct((rows, columns), jnp.bfloat16),
        scratch_shapes=[
            pltpu.VMEM((rows, depth), jnp.bfloat16),
            pltpu.VMEM((rows, depth), jnp.bfloat16),
            pltpu.VMEM((rows, tile), jnp.float32),
            pltpu.VMEM((rows, columns), jnp.bfloat16),
            pltpu.SemaphoreType.DMA((tiles,)),
            pltpu.VMEM((late, depth, tile), jnp.bfloat16),
            pltpu.SemaphoreType.DMA((late,)),
        ],
        compiler_params=pltpu.CompilerParams(vmem_limit_bytes=24 * MIB),
        cost_estimate=pl.CostEstimate(
            flops=4 * rows * depth * columns, bytes_accessed=32 * MIB, transcendentals=0
        ),
    )(*[in_vmem(x) for x in own + other], in_vmem(own_w), in_hbm(other_w), base, own_base, *ready)


def shards(queries, keys, values, segments, out_weight):
    rows = queries.shape[0]
    assert ATTENTION_SPAN == 2 * rows
    heads_kv = keys.shape[1] // HEAD_SIZE
    peers = lax.axis_size("seq")
    seq_index = lax.axis_index("seq")
    swap = [(0, 1), (1, 0)]

    own = list(pack(keys, values))
    out_weight, own[0] = lax.optimization_barrier((out_weight, own[0]))
    other_w = lax.ppermute(out_weight, "head", swap)
    two_on = [(i, i + 2) for i in range(peers - 2)]
    pair = [(i, i ^ 1) for i in range(peers)]
    odd = seq_index % 2 == 1
    far = [lax.ppermute(x, "seq", two_on) for x in own[:-1]]
    queries, segments, far[0] = lax.optimization_barrier((queries, segments, far[0]))
    marks, queries = prepare(seq_index.astype(jnp.int32).reshape(1), segments, queries)
    upper_w = out_weight
    upper_w, marks = lax.optimization_barrier((upper_w, marks))
    upper_w = stage(upper_w)
    far[2], upper_w = lax.optimization_barrier((far[2], upper_w))
    near = [lax.ppermute(jnp.where(odd, f, x), "seq", pair) for f, x in zip(far, own)]
    beside = lax.ppermute(own[-1], "seq", pair)
    last, far[0] = lax.optimization_barrier((jnp.concatenate([own[-1], beside]), far[0]))
    last = lax.ppermute(last, "seq", two_on)
    far.append(last[:rows])
    near.append(jnp.where(odd, beside, last[rows:]))

    mine, ready = [], []
    for h in range(heads_kv):
        if mine:
            marks, mine[-1] = lax.optimization_barrier((marks, mine[-1]))
        weights = other_w if h == heads_kv - 1 else None
        result, *tile = attend(queries, marks, h, (own[h], near[h], far[h]), weights)
        mine.append(result)
        ready += tile
        if h == heads_kv // 2 - 1:
            own_base = project_own(mine, upper_w, column_tile(out_weight.shape[1]))
            marks, own_base = lax.optimization_barrier((marks, own_base))
    theirs = [lax.ppermute(x, "head", swap) for x in mine]
    base = project_early(mine[:-1], theirs[:-1], out_weight, ready[0])
    return project(mine, theirs, out_weight, other_w, ready, base, own_base)


def solution(mesh):
    placed = (
        P(("groups", "seq"), "head"),
        P(("groups", "seq"), "head"),
        P(("groups", "seq"), "head"),
        P("groups"),
        P("head", None),
    )
    return jax.shard_map(
        shards, mesh=mesh, in_specs=placed, out_specs=P(("groups", "seq"), None), check_vma=False
    )
```

```python
import functools

import jax
import jax.numpy as jnp
from jax import lax
from jax.experimental import pallas as pl
from jax.experimental.pallas import tpu as pltpu
from jax.sharding import PartitionSpec as P

HEAD_SIZE = 128
SCALAR = 168
ATTENTION_SPAN = 1024
TILE = 128
MARK = 128.0
LOG2E = 1.4426950408889634
MIB = 1 << 20
EARLY = 2


def joined(*parts):
    parts = [part for part in parts if part.shape[1]]
    return parts[0] if len(parts) == 1 else jnp.concatenate(parts, axis=1)


def attend_kernel(q_ref, own_ref, near_ref, far_ref, mark_ref, out_ref):
    rows = own_ref.shape[0]
    group = q_ref.shape[1] // HEAD_SIZE
    factor = LOG2E * SCALAR ** (-0.5)
    ones = jnp.ones((rows, HEAD_SIZE), jnp.bfloat16)

    def keys_of(ref, block):
        marks = mark_ref[block * rows : (block + 1) * rows, :]
        return jnp.concatenate([ref[:, :HEAD_SIZE], marks], axis=1)

    def values_of(ref):
        return jnp.concatenate([ref[:, HEAD_SIZE:], ones], axis=1)

    keys = [keys_of(far_ref, 0), keys_of(near_ref, 1), keys_of(own_ref, 2)]
    values = [values_of(far_ref), values_of(near_ref), values_of(own_ref)]
    row = lax.broadcasted_iota(jnp.int32, (TILE, TILE), 0)
    col = lax.broadcasted_iota(jnp.int32, (TILE, TILE), 1)
    inside = jnp.concatenate([col > row] * group, axis=0)
    causal = jnp.concatenate([col <= row] * group, axis=0)

    def score_tile(t):
        span = slice(t * TILE, (t + 1) * TILE)
        marks = mark_ref[2 * rows + t * TILE : 2 * rows + (t + 1) * TILE, :]
        query = jnp.concatenate(
            [
                jnp.concatenate([q_ref[span, g * HEAD_SIZE : (g + 1) * HEAD_SIZE], marks], axis=1)
                for g in range(group)
            ],
            axis=0,
        )
        parts = [keys[0][t * TILE :], keys[1], keys[2][: (t + 1) * TILE]]
        scores = [
            lax.dot_general(
                query, key, (((1,), (1,)), ((), ())), preferred_element_type=jnp.float32
            )
            for key in parts
        ]
        first = jnp.where(inside, scores[0][:, :TILE], -1e30)
        scores[0] = joined(first, *([scores[0][:, TILE:]] if scores[0].shape[1] > TILE else []))
        last = jnp.where(causal, scores[2][:, t * TILE :], -1e30)
        scores[2] = joined(*([scores[2][:, : t * TILE]] if t else []), last)
        return scores

    def weigh_tile(t, scores):
        columns = [
            score[:, c : c + HEAD_SIZE]
            for score in scores
            for c in range(0, score.shape[1], HEAD_SIZE)
        ]
        top = jnp.max(functools.reduce(jnp.maximum, columns), axis=1, keepdims=True)
        return [jnp.exp2((score - top) * factor).astype(jnp.bfloat16) for score in scores]

    def give_tile(t, weights):
        span = slice(t * TILE, (t + 1) * TILE)
        parts = [values[0][t * TILE :], values[1], values[2][: (t + 1) * TILE]]
        total = None
        for weight, value in zip(weights, parts):
            term = jnp.dot(weight, value, preferred_element_type=jnp.float32)
            total = term if total is None else total + term
        result = (total[:, :HEAD_SIZE] / total[:, HEAD_SIZE:]).astype(jnp.bfloat16)
        for g in range(group):
            out_ref[span, g * HEAD_SIZE : (g + 1) * HEAD_SIZE] = result[
                g * TILE : (g + 1) * TILE
            ]

    tiles = rows // TILE
    scores = [score_tile(t) for t in range(tiles)]
    weights = [weigh_tile(t, scores[t]) for t in range(tiles)]
    for t in range(tiles):
        give_tile(t, weights[t])


def in_vmem(x):
    return pltpu.with_memory_space_constraint(x, pltpu.VMEM)


def in_hbm(x):
    return pltpu.with_memory_space_constraint(x, pltpu.HBM)


def pack_kernel(keys_ref, values_ref, *refs):
    outs, sem = refs[:-1], refs[-1]
    copies = []
    for h, out in enumerate(outs):
        for side, ref in enumerate((keys_ref, values_ref)):
            copies.append(
                pltpu.make_async_copy(
                    ref.at[:, h * HEAD_SIZE : (h + 1) * HEAD_SIZE],
                    out.at[:, side * HEAD_SIZE : (side + 1) * HEAD_SIZE],
                    sem.at[h, side],
                )
            )
    for copy in copies:
        copy.start()
    for copy in copies:
        copy.wait()


def pack(keys, values):
    rows, heads = keys.shape[0], keys.shape[1] // HEAD_SIZE
    return pl.pallas_call(
        pack_kernel,
        in_specs=[pl.BlockSpec(memory_space=pltpu.HBM)] * 2,
        out_specs=[pl.BlockSpec(memory_space=pltpu.VMEM)] * heads,
        out_shape=[pltpu.VMEM((rows, 2 * HEAD_SIZE), jnp.bfloat16)] * heads,
        scratch_shapes=[pltpu.SemaphoreType.DMA((heads, 2))],
        compiler_params=pltpu.CompilerParams(vmem_limit_bytes=2 * MIB),
        cost_estimate=pl.CostEstimate(flops=0, bytes_accessed=2 * MIB, transcendentals=0),
    )(in_hbm(keys), in_hbm(values))


def prepare(seq_index, segments, queries):
    rows = queries.shape[0]
    slab = segments.shape[0]
    blocks = 3

    def kernel(index_ref, seg_ref, q_ref, mark_ref, q_out, sem):
        copy = pltpu.make_async_copy(q_ref, q_out, sem)
        copy.start()
        ids = lax.broadcasted_iota(jnp.int32, (HEAD_SIZE, HEAD_SIZE), 0)
        pieces = rows // HEAD_SIZE
        for b in range(blocks):
            block = index_ref[0] + b - (blocks - 1)
            for p in range(pieces):
                seen = seg_ref[pl.ds(jnp.maximum(block, 0) * pieces + p, 1), :]
                hit = (seen == ids) & (block >= 0)
                mark = jnp.where(hit, MARK, 0.0)
                at = b * rows + p * HEAD_SIZE
                mark_ref[at : at + HEAD_SIZE, :] = mark.T.astype(jnp.bfloat16)
        copy.wait()

    vmem = pl.BlockSpec(memory_space=pltpu.VMEM)
    return pl.pallas_call(
        kernel,
        in_specs=[
            pl.BlockSpec(memory_space=pltpu.SMEM),
            vmem,
            pl.BlockSpec(memory_space=pltpu.HBM),
        ],
        out_specs=[vmem, vmem],
        out_shape=[
            pltpu.VMEM((blocks * rows, HEAD_SIZE), jnp.bfloat16),
            pltpu.VMEM(queries.shape, queries.dtype),
        ],
        scratch_shapes=[pltpu.SemaphoreType.DMA],
        compiler_params=pltpu.CompilerParams(vmem_limit_bytes=4 * MIB),
        cost_estimate=pl.CostEstimate(flops=1024, bytes_accessed=1024, transcendentals=0),
    )(seq_index, segments.reshape(slab // HEAD_SIZE, HEAD_SIZE), in_hbm(queries))


def column_tile(columns):
    return 768 if columns % 768 == 0 else 128


def tile_copy(weights, n, into, sem):
    tile = into.shape[1]
    place = pl.ds(pl.multiple_of(n * tile, tile), tile)
    return pltpu.make_async_copy(weights.at[:, place], into, sem)


def attend(queries, marks, head, part, weights=None):
    rows = marks.shape[0] // 3
    width = 2 * HEAD_SIZE

    def kernel(q_ref, mark_ref, own_ref, near_ref, far_ref, *refs):
        if weights is None:
            (out_ref,) = refs
        else:
            w_ref, out_ref, *tile_refs, sem = refs
            copies = [tile_copy(w_ref, n, ref, sem.at[n]) for n, ref in enumerate(tile_refs)]
            for copy in copies:
                copy.start()
        left = head * width
        attend_kernel(
            q_ref.at[:, left : left + width], own_ref, near_ref, far_ref, mark_ref, out_ref
        )
        if weights is not None:
            for copy in copies:
                copy.wait()

    vmem = pl.BlockSpec(memory_space=pltpu.VMEM)
    specs, outs = [vmem] * 5, [pltpu.VMEM((rows, width), jnp.bfloat16)]
    flat, scratch = [], []
    if weights is not None:
        depth, columns = weights.shape
        specs.append(pl.BlockSpec(memory_space=pltpu.HBM))
        flat.append(in_hbm(weights))
        outs += [pltpu.VMEM((depth, column_tile(columns)), jnp.bfloat16)] * EARLY
        scratch.append(pltpu.SemaphoreType.DMA((EARLY,)))
    return pl.pallas_call(
        kernel,
        in_specs=specs,
        out_specs=[vmem] * len(outs),
        out_shape=outs,
        scratch_shapes=scratch,
        compiler_params=pltpu.CompilerParams(vmem_limit_bytes=8 * MIB),
        cost_estimate=pl.CostEstimate(flops=1024, bytes_accessed=1024, transcendentals=0),
    )(queries, marks, *[in_vmem(x) for x in part], *flat)


def stage_kernel(in_ref, out_ref, sem, *, skip):
    rows, columns = out_ref.shape
    copy = pltpu.make_async_copy(in_ref.at[:rows, skip : skip + columns], out_ref, sem)
    copy.start()
    copy.wait()


def stage(own_w):
    depth, columns = own_w.shape
    skip = column_tile(columns)
    return pl.pallas_call(
        functools.partial(stage_kernel, skip=skip),
        in_specs=[pl.BlockSpec(memory_space=pltpu.HBM)],
        out_specs=pl.BlockSpec(memory_space=pltpu.VMEM),
        out_shape=pltpu.VMEM((depth // 2, columns - skip), own_w.dtype),
        scratch_shapes=[pltpu.SemaphoreType.DMA],
        compiler_params=pltpu.CompilerParams(vmem_limit_bytes=MIB),
        cost_estimate=pl.CostEstimate(flops=1024, bytes_accessed=1024, transcendentals=0),
    )(in_hbm(own_w))


def project_own(own, upper_w, tile):
    count = len(own)
    rows, width = own[0].shape
    columns = upper_w.shape[1]
    tile *= 2 if columns % (2 * tile) == 0 else 1
    depth = count * width

    def kernel(*refs):
        own_refs, (upper_w_ref, out_ref, row) = refs[:count], refs[count:]
        for i, ref in enumerate(own_refs):
            row[:, i * width : (i + 1) * width] = ref[...]

        for n in range(columns // tile):
            place = slice(n * tile, (n + 1) * tile)
            out_ref[:, place] = jnp.dot(
                row[...], upper_w_ref[:, place], preferred_element_type=jnp.float32
            )

    vmem = pl.BlockSpec(memory_space=pltpu.VMEM)
    return pl.pallas_call(
        kernel,
        in_specs=[vmem] * (count + 1),
        out_specs=vmem,
        out_shape=pltpu.VMEM((rows, columns), jnp.float32),
        scratch_shapes=[pltpu.VMEM((rows, depth), jnp.bfloat16)],
        compiler_params=pltpu.CompilerParams(vmem_limit_bytes=10 * MIB),
        cost_estimate=pl.CostEstimate(flops=1024, bytes_accessed=1024, transcendentals=0),
    )(*[in_vmem(x) for x in own], upper_w)


def project_early(own, other, own_w, ready):
    count = len(own)
    rows, width = own[0].shape
    tile = ready.shape[1]
    depth = count * width

    def kernel(*refs):
        own_refs, other_refs = refs[:count], refs[count : 2 * count]
        own_w_ref, ready_ref, out_ref, row, other_row, other_sum = refs[2 * count :]
        for into, group in ((row, own_refs), (other_row, other_refs)):
            for i, ref in enumerate(group):
                into[:, i * width : (i + 1) * width] = ref[...]
        out_ref[...] = jnp.dot(
            row[...], own_w_ref[:depth, :tile], preferred_element_type=jnp.float32
        )
        other_sum[...] = jnp.dot(
            other_row[...], ready_ref[:depth, :], preferred_element_type=jnp.float32
        )
        out_ref[...] = out_ref[...] + other_sum[...]

    vmem = pl.BlockSpec(memory_space=pltpu.VMEM)
    return pl.pallas_call(
        kernel,
        in_specs=[vmem] * (2 * count + 2),
        out_specs=vmem,
        out_shape=pltpu.VMEM((rows, tile), jnp.float32),
        scratch_shapes=[pltpu.VMEM((rows, depth), jnp.bfloat16)] * 2
        + [pltpu.VMEM((rows, tile), jnp.float32)],
        compiler_params=pltpu.CompilerParams(vmem_limit_bytes=8 * MIB),
        cost_estimate=pl.CostEstimate(
            flops=4 * rows * depth * tile, bytes_accessed=4 * MIB, transcendentals=0
        ),
    )(*[in_vmem(x) for x in own + other], in_vmem(own_w), ready)


def project(own, other, own_w, other_w, ready, base, own_base):
    count = len(own)
    rows = own[0].shape[0]
    depth, columns = own_w.shape
    tile = column_tile(columns)
    tiles = columns // tile
    late = tiles - len(ready)

    def kernel(*refs):
        own_refs, other_refs = refs[:count], refs[count : 2 * count]
        own_w_ref, other_w_ref, *refs = refs[2 * count :]
        base_ref, own_base_ref, *refs = refs
        ready_refs, refs = refs[: len(ready)], refs[len(ready) :]
        out_ref, row, other_row, own_sum, other_base, held, out_sem, w_buf, w_sem = refs

        def place(n):
            return pl.ds(pl.multiple_of(n * tile, tile), tile)

        def give(n):
            return pltpu.make_async_copy(
                held.at[:, place(n)], out_ref.at[:, place(n)], out_sem.at[n]
            )

        def coming(n):
            slot = n - len(ready)
            return tile_copy(other_w_ref, n, w_buf.at[slot], w_sem.at[slot])

        def dot(array, weight, down, place=slice(None)):
            return jnp.dot(
                array[:, down], weight[down, place], preferred_element_type=jnp.float32
            )

        def finish(n, total):
            held[:, place(n)] = total.astype(held.dtype)
            give(n).start()

        def multiply_first(weight):
            down = slice(depth - own_refs[-1].shape[1], depth)
            own_sum[...] = dot(row, own_w_ref, down, place(0))
            other_base[...] = dot(other_row, weight, down)
            finish(0, (own_sum[...] + other_base[...]) + base_ref[...])

        def multiply(n, weight):
            half, rest = slice(0, depth // 2), slice(depth // 2, depth)
            other_base[...] = dot(other_row, weight, half)
            own_sum[...] = own_base_ref[:, place(n - 1)] + dot(row, own_w_ref, rest, place(n))
            other_base[...] = other_base[...] + dot(other_row, weight, rest)
            finish(n, own_sum[...] + other_base[...])

        for n in range(len(ready), tiles):
            coming(n).start()
        for into, group in ((row, own_refs), (other_row, other_refs)):
            for i, ref in enumerate(group):
                width = ref.shape[1]
                into[:, i * width : (i + 1) * width] = ref[...]
        for n, ref in enumerate(ready_refs):
            if n:
                multiply(n, ref)
            else:
                multiply_first(ref)

        @pl.loop(len(ready), tiles)
        def _(n):
            coming(n).wait()
            multiply(n, w_buf.at[n - len(ready)])

        @pl.loop(0, tiles)
        def _(n):
            give(n).wait()

    vmem = pl.BlockSpec(memory_space=pltpu.VMEM)
    hbm = pl.BlockSpec(memory_space=pltpu.HBM)
    return pl.pallas_call(
        kernel,
        in_specs=[vmem] * (2 * count + 1) + [hbm] + [vmem] * (2 + len(ready)),
        out_specs=pl.BlockSpec(memory_space=pl.ANY),
        out_shape=jax.ShapeDtypeStruct((rows, columns), jnp.bfloat16),
        scratch_shapes=[
            pltpu.VMEM((rows, depth), jnp.bfloat16),
            pltpu.VMEM((rows, depth), jnp.bfloat16),
            pltpu.VMEM((rows, tile), jnp.float32),
            pltpu.VMEM((rows, tile), jnp.float32),
            pltpu.VMEM((rows, columns), jnp.bfloat16),
            pltpu.SemaphoreType.DMA((tiles,)),
            pltpu.VMEM((late, depth, tile), jnp.bfloat16),
            pltpu.SemaphoreType.DMA((late,)),
        ],
        compiler_params=pltpu.CompilerParams(vmem_limit_bytes=26 * MIB),
        cost_estimate=pl.CostEstimate(
            flops=4 * rows * depth * columns, bytes_accessed=32 * MIB, transcendentals=0
        ),
    )(*[in_vmem(x) for x in own + other], in_vmem(own_w), in_hbm(other_w), base, own_base, *ready)


def shards(queries, keys, values, segments, out_weight):
    rows = queries.shape[0]
    assert ATTENTION_SPAN == 2 * rows
    heads_kv = keys.shape[1] // HEAD_SIZE
    peers = lax.axis_size("seq")
    seq_index = lax.axis_index("seq")
    swap = [(0, 1), (1, 0)]

    own = list(pack(keys, values))
    out_weight, own[0] = lax.optimization_barrier((out_weight, own[0]))
    other_w = lax.ppermute(out_weight, "head", swap)
    two_on = [(i, i + 2) for i in range(peers - 2)]
    pair = [(i, i ^ 1) for i in range(peers)]
    odd = seq_index % 2 == 1
    far = [lax.ppermute(x, "seq", two_on) for x in own[:-1]]
    queries, segments, far[0] = lax.optimization_barrier((queries, segments, far[0]))
    marks, queries = prepare(seq_index.astype(jnp.int32).reshape(1), segments, queries)
    upper_w = out_weight
    upper_w, marks = lax.optimization_barrier((upper_w, marks))
    upper_w = stage(upper_w)
    far[2], upper_w = lax.optimization_barrier((far[2], upper_w))
    near = [lax.ppermute(jnp.where(odd, f, x), "seq", pair) for f, x in zip(far, own)]
    beside = lax.ppermute(own[-1], "seq", pair)
    last, far[0] = lax.optimization_barrier((jnp.concatenate([own[-1], beside]), far[0]))
    last = lax.ppermute(last, "seq", two_on)
    far.append(last[:rows])
    near.append(jnp.where(odd, beside, last[rows:]))

    mine, ready = [], []
    for h in range(heads_kv):
        if mine:
            marks, mine[-1] = lax.optimization_barrier((marks, mine[-1]))
        weights = other_w if h == heads_kv - 1 else None
        result, *tile = attend(queries, marks, h, (own[h], near[h], far[h]), weights)
        mine.append(result)
        ready += tile
        if h == heads_kv // 2 - 1:
            own_base = project_own(mine, upper_w, column_tile(out_weight.shape[1]))
            marks, own_base = lax.optimization_barrier((marks, own_base))
    theirs = [lax.ppermute(x, "head", swap) for x in mine]
    base = project_early(mine[:-1], theirs[:-1], out_weight, ready[0])
    return project(mine, theirs, out_weight, other_w, ready, base, own_base)


def solution(mesh):
    placed = (
        P(("groups", "seq"), "head"),
        P(("groups", "seq"), "head"),
        P(("groups", "seq"), "head"),
        P("groups"),
        P("head", None),
    )
    return jax.shard_map(
        shards, mesh=mesh, in_specs=placed, out_specs=P(("groups", "seq"), None), check_vma=False
    )
```
